32 devices in a mesh: rows: 16 (over z, y, x), probes: 2 (over core).
Axes of the slice: x: 2, y: 2, z: 4, core: 2. Of those that a mesh axis runs over, the one named last changes fastest.
Arguments:
- probes: bfloat16 [32, 16, 256], P('rows', 'probes'), parts along dimension 1, may hold values from -6 to 6
- factor: bfloat16 [32, 4, 256, 256], P('rows'), may hold values from -0.125 to 0.125
- inverses: bfloat16 [32, 256, 256], P('rows')
- pattern: int32 [32, 4], replicated, may hold values from -1 to 23, as said below
- owner: int32 [32], replicated, may hold values from 0 to 31, each once
Outputs:
- solution: bfloat16 [32, 16, 256], P('rows', 'probes'), parts along dimension 1
- selected: bfloat16 [32, 10, 256, 256], P('rows', 'probes'), parts along dimension 1
The draws below stay inside these ranges and needn't reach their ends.
There are 2 independent parts, one for each index of `probes`. The reference program is written for one: setup_inputs(seed, part) draws one part's arguments, and reference() takes and returns one part's arrays. A program takes and returns all parts, laid end to end along the dimension named above; an argument that names none is the same for every part. Nothing has to cross between parts.
Inputs may be any that keep to these rules, and one draw needn't show every extreme that they name: `pattern`: Block-rows of the first level have only -1; every other block-row i names 4 different block-columns, all in levels below the level of i, one of them the block-row just before the first block-row of its own level.
All inputs are finite; a program needn't handle non-finite values.
Results may differ from the reference program's by a relative error of at most 0.012.
Values may be sent and summed in bfloat16 or wider, within the bound.
A program may use at most 64 MiB of HBM per device.

```python
import math
import jax
import jax.numpy as jnp
from jax import lax

BLOCK = 256
PROBES = 8
ROWS_DEV = 2
NEIGHBORS = 4
LEVELS = 4
N_BLOCKROWS = 32


def draw_inverses(key, part):
    key = jax.random.fold_in(key, 23)
    first, second = jax.random.split(key)
    diag = jax.random.uniform(first, (N_BLOCKROWS, BLOCK), minval=0.6, maxval=1.0)
    off = jax.random.normal(second, (N_BLOCKROWS, BLOCK, BLOCK)) * (0.35 / math.sqrt(BLOCK))
    eye = jnp.eye(BLOCK, dtype=jnp.float32)
    return (off + eye[None] * diag[:, :, None]).astype(jnp.bfloat16)


def draw_pattern(key, part):
    key = jax.random.fold_in(key, 11)
    width = N_BLOCKROWS // LEVELS
    rows_all = jnp.arange(N_BLOCKROWS, dtype=jnp.int32)
    limits = rows_all // width * width
    keys = jax.random.split(key, N_BLOCKROWS)

    def one_row(row_key, limit):
        scores = jax.random.permutation(row_key, N_BLOCKROWS).astype(jnp.int32)
        masked = jnp.where(rows_all < limit, scores, scores + N_BLOCKROWS)
        masked = jnp.where(rows_all == limit - 1, -1, masked).astype(jnp.int32)
        picked = lax.top_k(-masked, NEIGHBORS)[1].astype(jnp.int32)
        return jnp.where(limit > 0, picked, -1).astype(jnp.int32)
    return jax.vmap(one_row)(keys, limits)


def steps_of(key, shape, cuts, least, top_value):
    def one(axis_at, parts):
        draws = jax.random.uniform(jax.random.fold_in(jax.random.fold_in(key, 6), axis_at), (parts,), jnp.float32, least / len(cuts), top_value / len(cuts))
        return jnp.repeat(jnp.exp(draws), shape[axis_at] // parts).reshape((-1,) + (1,) * (len(shape) - axis_at - 1))

    level = one(*cuts[0])
    for cut in cuts[1:]:
        level = level * one(*cut)
    return level


def scatter_about(stream_key, shape, spread, most, cuts=(), kind=jnp.bfloat16):
    values = jax.random.normal(stream_key, shape, jnp.float32) * spread
    if len(cuts) > 0:
        values = steps_of(stream_key, shape, cuts, -0.22, 0.18) * values
    return jnp.clip(values, min=-most, max=most).astype(kind)


def setup_inputs(seed: int = 0, part: int = 0) -> dict:
    arg_keys = jax.random.split(jax.random.key(seed), 6)
    own_keys = jax.random.split(jax.random.fold_in(arg_keys[5], part), 6)
    probes = scatter_about(own_keys[0], (N_BLOCKROWS, PROBES, BLOCK), 1.0, 6.0, ((0, 16),))
    factor = scatter_about(arg_keys[1], (N_BLOCKROWS, NEIGHBORS, BLOCK, BLOCK), (2 * BLOCK * NEIGHBORS) ** -0.5, 0.125, ((0, 16),))
    inverses = draw_inverses(jax.random.fold_in(arg_keys[5], 71), part)
    pattern = draw_pattern(jax.random.fold_in(arg_keys[5], 71), part)
    owner = jax.random.permutation(arg_keys[4], N_BLOCKROWS).astype(jnp.int32)
    return {"probes": probes, "factor": factor, "inverses": inverses, "pattern": pattern, "owner": owner}


def reference(probes, factor, inverses, pattern, owner):
    f32 = jnp.float32
    bf16 = jnp.bfloat16
    groups = N_BLOCKROWS // ROWS_DEV
    width = N_BLOCKROWS // LEVELS
    solved = jnp.zeros((N_BLOCKROWS, PROBES, BLOCK), bf16)
    for row in range(N_BLOCKROWS):
        slot = owner[row]
        cols = pattern[row]
        valid = cols >= 0
        safe = jnp.maximum(cols, 0).astype(jnp.int32)
        near = jnp.where(valid[:, None, None], solved[safe].astype(f32), jnp.zeros((), f32))
        partial_value = jnp.einsum("kpb,kab->pa", near, factor[slot].astype(f32))
        resid = (probes[slot].astype(f32) - partial_value).astype(bf16)
        value = jnp.dot(resid, inverses[slot].T, preferred_element_type=f32).astype(bf16)
        solved = solved.at[row].set(value)
    accum = jnp.zeros((N_BLOCKROWS, PROBES, BLOCK), f32)
    backed = jnp.zeros((N_BLOCKROWS, PROBES, BLOCK), bf16)
    for level in range(LEVELS - 1, -1, -1):
        rows_now = jnp.arange(level * width, (level + 1) * width, dtype=jnp.int32)
        slots = owner[rows_now]
        start = (solved[rows_now].astype(f32) - accum[rows_now]).astype(bf16)
        value = jnp.einsum("rpb,rba->rpa", start.astype(f32), inverses[slots].astype(f32)).astype(bf16)
        backed = backed.at[rows_now].set(value)
        if level > 0:
            cols = pattern[rows_now]
            valid = cols >= 0
            safe = jnp.maximum(cols, 0).astype(jnp.int32)
            terms = jnp.einsum("rpa,rkab->rkpb", value.astype(f32), factor[slots].astype(f32))
            terms = jnp.where(valid[:, :, None, None], terms, jnp.zeros((), f32))
            group = (slots // ROWS_DEV).astype(jnp.int32)
            group_all = jnp.broadcast_to(group[:, None], safe.shape)
            part = jnp.zeros((groups, N_BLOCKROWS, PROBES, BLOCK), f32).at[group_all, safe].add(terms)
            accum = accum + jnp.sum(part, axis=0)
    solution = jnp.zeros_like(backed).at[owner].set(backed)
    ordered = probes[owner]

    def one_row(row):
        cols = pattern[row]
        valid = cols >= 0
        safe = jnp.maximum(cols, 0).astype(jnp.int32)
        near = jnp.where(valid[:, None, None], ordered[safe].astype(f32), jnp.zeros((), f32))
        value = backed[row].astype(f32)
        off = jnp.einsum("pa,kpb->kab", value, near)
        diag = jnp.einsum("pa,pb->ab", value, ordered[row].astype(f32))
        return (jnp.concatenate([off, diag[None]], axis=0) / PROBES).astype(bf16)

    blocks = lax.map(one_row, jnp.arange(N_BLOCKROWS, dtype=jnp.int32))
    selected = jnp.zeros_like(blocks).at[owner].set(blocks)
    return solution, selected
```

```python
import functools

import jax
import jax.numpy as jnp
from jax import lax
from jax.experimental import pallas as pl
from jax.experimental.pallas import tpu as pltpu
from jax.sharding import PartitionSpec as P

LEVELS = 4
ROUNDS = LEVELS - 1
MESH = pl.DeviceIdType.MESH
F32 = jnp.float32
BF16 = jnp.bfloat16


def dot_nt(a, b):
    return lax.dot_general(a, b, (((1,), (1,)), ((), ())), preferred_element_type=F32)


def dot_nn(a, b):
    return lax.dot_general(a, b, (((1,), (0,)), ((), ())), preferred_element_type=F32)


def dot_tn(a, b):
    return lax.dot_general(a, b, (((0,), (0,)), ((), ())), preferred_element_type=F32)


def solve_kernel(n, local, count, neighbors, total, *refs):
    probes_ref, factor_hbm, inv_hbm, pattern_ref, owner_ref = refs[:5]
    back_ref, near_ref = refs[5:7]
    scratch = refs[7:]
    factor_ref, inv_ref, terms_ref, table_ref, all_probes = scratch[:5]
    ahead = scratch[5 : 5 + ROUNDS]
    outs = scratch[5 + ROUNDS : 5 + 2 * ROUNDS]
    arrive = scratch[5 + 2 * ROUNDS : 5 + 3 * ROUNDS]
    load_sem, send_sem, recv_sem = scratch[5 + 3 * ROUNDS :]
    me = lax.axis_index("rows")

    load_inv = pltpu.make_async_copy(inv_hbm, inv_ref, load_sem.at[0])
    load_factor = pltpu.make_async_copy(factor_hbm, factor_ref, load_sem.at[1])
    load_inv.start()
    load_factor.start()

    def peer(step):
        return lax.rem(me + step, n)

    barrier = pltpu.get_barrier_semaphore()

    def greet(step, carry):
        pl.semaphore_signal(barrier, inc=1, device_id={"rows": peer(step)}, device_id_type=MESH)
        return carry

    lax.fori_loop(1, n, greet, 0)

    def halves(block):
        wide = block.astype(F32)
        return [wide[r * count : (r + 1) * count] for r in range(local)]

    def pick(ref, slot, valid):
        parts = halves(ref[lax.div(slot, local)])
        at = lax.rem(slot, local)
        value = parts[0]
        for r in range(1, local):
            value = jnp.where(at == r, parts[r], value)
        return jnp.where(valid, value, jnp.zeros_like(value)).astype(BF16)

    def send(ref, step, at):
        to = peer(step)
        return pltpu.make_async_remote_copy(
            src_ref=ref[0].at[ref[1](to)],
            dst_ref=ref[2].at[me],
            send_sem=send_sem.at[at],
            recv_sem=recv_sem.at[at],
            device_id={"rows": to},
            device_id_type=MESH,
        )

    def whole_of(ref, at):
        every = ref.at[pl.ds(0, n - 1)]
        return pltpu.make_async_remote_copy(
            src_ref=every,
            dst_ref=every,
            send_sem=send_sem.at[at],
            recv_sem=recv_sem.at[at],
            device_id={"rows": peer(1)},
            device_id_type=MESH,
        )

    def broadcast(ref, at):
        def one(step, carry):
            send((ref, lambda to: me, ref), step, at).start()
            return carry

        lax.fori_loop(1, n, one, 0)

    probes = [probes_ref[r] for r in range(local)]
    probes_wide = [p.astype(F32) for p in probes]

    load_inv.wait()

    def solve_ahead(resid):
        return [dot_nt(resid[r], inv_ref[r]).astype(BF16) for r in range(local)]

    def store_rows(ref, at, values):
        ref[at] = jnp.concatenate([v.astype(F32) for v in values], axis=0).astype(BF16)

    solved = solve_ahead(probes)
    store_rows(ahead[0], me, solved)
    store_rows(all_probes, me, probes)

    pl.semaphore_wait(barrier, n - 1)
    broadcast(ahead[0], 0)
    broadcast(all_probes, 2 * ROUNDS)

    sources, valids = [], []
    for r in range(local):
        slot = me * local + r
        row = lax.fori_loop(
            0, total, lambda i, found: jnp.where(owner_ref[i] == slot, i, found), 0, unroll=8
        )
        cols = [pattern_ref[row, k] for k in range(neighbors)]
        valids.append([c >= 0 for c in cols])
        sources.append([owner_ref[jnp.maximum(c, 0)] for c in cols])

    def fill(slot, carry):
        for r in range(local):
            found = neighbors
            for k in range(neighbors):
                here = jnp.logical_and(sources[r][k] == slot, valids[r][k])
                found = jnp.where(here, k, found)
            table_ref[r, slot] = found
        return carry

    lax.fori_loop(0, total, fill, 0)
    for r in range(local):
        terms_ref[r, neighbors] = jnp.zeros((count, probes_wide[0].shape[1]), F32)

    load_factor.wait()

    for level in range(1, LEVELS):
        whole_of(ahead[level - 1], level - 1).wait_recv()
        resid = []
        for r in range(local):
            total_value = jnp.zeros_like(probes_wide[r])
            for k in range(neighbors):
                near = pick(ahead[level - 1], sources[r][k], valids[r][k])
                total_value += dot_nt(near, factor_ref[r, k])
            resid.append((probes_wide[r] - total_value).astype(BF16))
        solved = solve_ahead(resid)
        if level < ROUNDS:
            store_rows(ahead[level], me, solved)
            broadcast(ahead[level], level)

    solved_wide = [v.astype(F32) for v in solved]
    start = solved
    for turn in range(LEVELS):
        backed = [dot_nn(start[r], inv_ref[r]).astype(BF16) for r in range(local)]
        if turn == ROUNDS:
            break
        for r in range(local):
            for k in range(neighbors):
                terms_ref[r, k] = dot_nn(backed[r], factor_ref[r, k])

        def part(device):
            rows = []
            for q in range(local):
                slot = device * local + q
                value = terms_ref[0, table_ref[0, slot]]
                for r in range(1, local):
                    value += terms_ref[r, table_ref[r, slot]]
                rows.append(value)
            return jnp.concatenate(rows, axis=0).astype(BF16)

        out, into, at = outs[turn], arrive[turn], ROUNDS + turn

        def one(step, carry):
            to = peer(step)
            out[to] = part(to)
            send((out, lambda d: d, into), step, at).start()
            return carry

        lax.fori_loop(1, n, one, 0)
        into[me] = part(me)
        whole_of(into, at).wait_recv()
        acc = lax.fori_loop(
            1, n, lambda d, sum_: sum_ + into[d].astype(F32), into[0].astype(F32), unroll=True
        )
        start = [
            (solved_wide[r] - acc[r * count : (r + 1) * count]).astype(BF16) for r in range(local)
        ]

    whole_of(all_probes, 2 * ROUNDS).wait_recv()
    for r in range(local):
        back_ref[r] = backed[r]
        width = probes_wide[r].shape[1]
        for k in range(neighbors):
            near_ref[r, :, k * width : (k + 1) * width] = pick(
                all_probes, sources[r][k], valids[r][k]
            )
        near_ref[r, :, neighbors * width :] = probes[r]

    for level in range(ROUNDS):
        whole_of(ahead[level], level).wait_send()
        whole_of(outs[level], ROUNDS + level).wait_send()
    whole_of(all_probes, 2 * ROUNDS).wait_send()


def select_kernel(local, count, blocks, back_ref, near_ref, sol_ref, sel_hbm, sel_ref, sems):
    copies = []
    width = back_ref.shape[2]
    for r in range(local):
        value = back_ref[r]
        sol_ref[r] = value
        near = near_ref[r]
        for k in range(blocks):
            product = dot_tn(value, near[:, k * width : (k + 1) * width])
            sel_ref[r, k] = (product / count).astype(BF16)
        copy = pltpu.make_async_copy(sel_ref.at[r], sel_hbm.at[r], sems.at[r])
        copy.start()
        copies.append(copy)
    for copy in copies:
        copy.wait()


def solution(mesh):
    n = mesh.shape["rows"]

    def body(probes, factor, inverses, pattern, owner):
        local, count, width = probes.shape
        neighbors = factor.shape[1]
        total = owner.shape[0]
        rows = local * count
        vmem = pl.BlockSpec(memory_space=pltpu.VMEM)
        smem = pl.BlockSpec(memory_space=pltpu.SMEM)
        anywhere = pl.BlockSpec(memory_space=pl.ANY)
        gathered = pltpu.VMEM((n, rows, width), BF16)
        backed, near = pl.pallas_call(
            functools.partial(solve_kernel, n, local, count, neighbors, total),
            out_shape=(
                jax.ShapeDtypeStruct((local, count, width), BF16),
                jax.ShapeDtypeStruct((local, count, (neighbors + 1) * width), BF16),
            ),
            in_specs=[vmem, anywhere, anywhere, smem, smem],
            out_specs=(vmem, vmem),
            scratch_shapes=[
                pltpu.VMEM(factor.shape, BF16),
                pltpu.VMEM(inverses.shape, BF16),
                pltpu.VMEM((local, neighbors + 1, count, width), F32),
                pltpu.SMEM((local, total), jnp.int32),
                gathered,
            ]
            + [gathered] * (3 * ROUNDS)
            + [
                pltpu.SemaphoreType.DMA((2,)),
                pltpu.SemaphoreType.DMA((2 * ROUNDS + 1,)),
                pltpu.SemaphoreType.DMA((2 * ROUNDS + 1,)),
            ],
            compiler_params=pltpu.CompilerParams(
                collective_id=0, has_side_effects=True, vmem_limit_bytes=40 * 1024 * 1024
            ),
            name="solve_rounds",
        )(probes, factor, inverses, pattern, owner)
        sol, selected = pl.pallas_call(
            functools.partial(select_kernel, local, count, neighbors + 1),
            out_shape=(
                jax.ShapeDtypeStruct((local, count, width), BF16),
                jax.ShapeDtypeStruct((local, neighbors + 1, width, width), BF16),
            ),
            in_specs=[vmem, vmem],
            out_specs=(vmem, anywhere),
            scratch_shapes=[
                pltpu.VMEM((local, neighbors + 1, width, width), BF16),
                pltpu.SemaphoreType.DMA((local,)),
            ],
            compiler_params=pltpu.CompilerParams(vmem_limit_bytes=16 * 1024 * 1024),
            name="select_blocks",
        )(backed, near)
        return sol, selected

    return jax.shard_map(
        body,
        mesh=mesh,
        in_specs=(
            P("rows", "probes", None),
            P("rows", None, None, None),
            P("rows", None, None),
            P(),
            P(),
        ),
        out_specs=(P("rows", "probes", None), P("rows", "probes", None, None)),
        check_vma=False,
    )
```

```python
import functools

import jax
import jax.numpy as jnp
from jax import lax
from jax.experimental import pallas as pl
from jax.experimental.pallas import tpu as pltpu
from jax.sharding import PartitionSpec as P

LEVELS = 4
ROUNDS = LEVELS - 1
MESH = pl.DeviceIdType.MESH
F32 = jnp.float32
BF16 = jnp.bfloat16


def dot_nt(a, b):
    return lax.dot_general(a, b, (((1,), (1,)), ((), ())), preferred_element_type=F32)


def dot_nn(a, b):
    return lax.dot_general(a, b, (((1,), (0,)), ((), ())), preferred_element_type=F32)


def dot_tn(a, b):
    return lax.dot_general(a, b, (((0,), (0,)), ((), ())), preferred_element_type=F32)


def solve_kernel(n, local, count, neighbors, total, *refs):
    probes_ref, factor_hbm, inv_hbm, pattern_ref, owner_ref = refs[:5]
    back_ref, near_ref = refs[5:7]
    scratch = refs[7:]
    factor_ref, inv_ref, factor_t, inv_t, terms_ref, table_ref, all_probes = scratch[:7]
    ahead = scratch[7 : 7 + ROUNDS]
    outs = scratch[7 + ROUNDS : 7 + 2 * ROUNDS]
    arrive = scratch[7 + 2 * ROUNDS : 7 + 3 * ROUNDS]
    load_sem, send_sem, recv_sem = scratch[7 + 3 * ROUNDS :]
    unroll = n <= 16
    group = max(g for g in range(1, 6) if (n - 1) % g == 0)
    me = lax.axis_index("rows")

    load_inv = pltpu.make_async_copy(inv_hbm, inv_ref, load_sem.at[0])
    load_factor = pltpu.make_async_copy(factor_hbm, factor_ref, load_sem.at[1])
    load_inv.start()
    load_factor.start()

    def peer(step):
        odd = step % 2
        away = n // 2 + odd * ((step + 1) // 2) - (1 - odd) * (step // 2)
        return lax.rem(me + away, n)

    barrier = pltpu.get_barrier_semaphore()

    def greet(step, carry):
        pl.semaphore_signal(barrier, inc=1, device_id={"rows": peer(step)}, device_id_type=MESH)
        return carry

    lax.fori_loop(0, n - 1, greet, 0, unroll=unroll)

    def halves(block):
        wide = block.astype(F32)
        return [wide[r * count : (r + 1) * count] for r in range(local)]

    def pick(ref, slot, valid):
        parts = halves(ref[lax.div(slot, local)])
        at = lax.rem(slot, local)
        value = parts[0]
        for r in range(1, local):
            value = jnp.where(at == r, parts[r], value)
        return jnp.where(valid, value, jnp.zeros_like(value)).astype(BF16)

    def send(ref, step, at):
        to = peer(step)
        return pltpu.make_async_remote_copy(
            src_ref=ref[0].at[ref[1](to)],
            dst_ref=ref[2].at[me],
            send_sem=send_sem.at[at],
            recv_sem=recv_sem.at[at],
            device_id={"rows": to},
            device_id_type=MESH,
        )

    def whole_of(ref, at):
        every = ref.at[pl.ds(0, n - 1)]
        return pltpu.make_async_remote_copy(
            src_ref=every,
            dst_ref=every,
            send_sem=send_sem.at[at],
            recv_sem=recv_sem.at[at],
            device_id={"rows": peer(0)},
            device_id_type=MESH,
        )

    def broadcast(ref, at, first=0, last=n - 1):
        def one(step, carry):
            send((ref, lambda to: me, ref), step, at).start()
            return carry

        lax.fori_loop(first, last, one, 0, unroll=unroll)

    def share_probes(turn):
        pieces = 2 * ROUNDS - 1
        size = -(-(n - 1) // pieces)
        first = min(turn * size, n - 1)
        last = min(first + size, n - 1)
        if last > first:
            broadcast(all_probes, 2 * ROUNDS, first, last)

    probes = [probes_ref[r] for r in range(local)]
    probes_wide = [p.astype(F32) for p in probes]

    load_inv.wait()

    def store_rows(ref, at, values):
        ref[at] = jnp.concatenate([v.astype(F32) for v in values], axis=0).astype(BF16)

    solved = [dot_nt(probes[r], inv_ref[r]).astype(BF16) for r in range(local)]
    store_rows(ahead[0], me, solved)
    store_rows(all_probes, me, probes)

    pl.semaphore_wait(barrier, n - 1)
    broadcast(ahead[0], 0)

    sources, valids = [], []
    for r in range(local):
        slot = me * local + r
        row = lax.fori_loop(
            0, total, lambda i, found: jnp.where(owner_ref[i] == slot, i, found), 0, unroll=8
        )
        cols = [pattern_ref[k, row] for k in range(neighbors)]
        valids.append([c >= 0 for c in cols])
        sources.append([owner_ref[jnp.maximum(c, 0)] for c in cols])

    def fill(slot, carry):
        for r in range(local):
            found = neighbors
            for k in range(neighbors):
                here = jnp.logical_and(sources[r][k] == slot, valids[r][k])
                found = jnp.where(here, k, found)
            table_ref[r, slot] = found
        return carry

    lax.fori_loop(0, total, fill, 0, unroll=4)
    for r in range(local):
        terms_ref[r, neighbors] = jnp.zeros((count, probes_wide[0].shape[1]), F32)

    load_factor.wait()
    for r in range(local):
        inv_t[r] = inv_ref[r].T
        for k in range(neighbors):
            factor_t[r, k] = factor_ref[r, k].T

    for level in range(1, LEVELS):
        whole_of(ahead[level - 1], level - 1).wait_recv()
        share_probes(level - 1)
        resid = []
        for r in range(local):
            total_value = jnp.zeros_like(probes_wide[r])
            for k in range(neighbors):
                near = pick(ahead[level - 1], sources[r][k], valids[r][k])
                total_value += dot_nn(near, factor_t[r, k])
            resid.append((probes_wide[r] - total_value).astype(BF16))
        solved = [dot_nn(resid[r], inv_t[r]).astype(BF16) for r in range(local)]
        if level < ROUNDS:
            store_rows(ahead[level], me, solved)
            broadcast(ahead[level], level)

    solved_wide = [v.astype(F32) for v in solved]
    start = solved
    for turn in range(LEVELS):
        backed = [dot_nn(start[r], inv_ref[r]).astype(BF16) for r in range(local)]
        if turn == ROUNDS:
            break
        for r in range(local):
            for k in range(neighbors):
                terms_ref[r, k] = dot_nn(backed[r], factor_ref[r, k])

        def part(device):
            rows = []
            for q in range(local):
                slot = device * local + q
                value = terms_ref[0, table_ref[0, slot]]
                for r in range(1, local):
                    value += terms_ref[r, table_ref[r, slot]]
                rows.append(value)
            return jnp.concatenate(rows, axis=0).astype(BF16)

        out, into, at = outs[turn], arrive[turn], ROUNDS + turn

        def some(chunk, carry):
            steps = [chunk * group + i for i in range(group)]
            values = [part(peer(step)) for step in steps]
            for step, value in zip(steps, values):
                out[peer(step)] = value
            for step in steps:
                send((out, lambda d: d, into), step, at).start()
            return carry

        lax.fori_loop(0, (n - 1) // group, some, 0, unroll=unroll)
        into[me] = part(me)
        whole_of(into, at).wait_recv()
        if turn < ROUNDS - 1:
            share_probes(ROUNDS + turn)
        acc = lax.fori_loop(
            1, n, lambda d, sum_: sum_ + into[d].astype(F32), into[0].astype(F32), unroll=True
        )
        start = [
            (solved_wide[r] - acc[r * count : (r + 1) * count]).astype(BF16) for r in range(local)
        ]

    whole_of(all_probes, 2 * ROUNDS).wait_recv()
    for r in range(local):
        back_ref[r] = backed[r]
        width = probes_wide[r].shape[1]
        for k in range(neighbors):
            near_ref[r, :, k * width : (k + 1) * width] = pick(
                all_probes, sources[r][k], valids[r][k]
            )
        near_ref[r, :, neighbors * width :] = probes[r]

    for level in range(ROUNDS):
        whole_of(ahead[level], level).wait_send()
        whole_of(outs[level], ROUNDS + level).wait_send()
    whole_of(all_probes, 2 * ROUNDS).wait_send()


def select_kernel(local, count, blocks, back_ref, near_ref, sol_ref, sel_hbm, sel_ref, sems):
    copies = []
    width = back_ref.shape[2]
    for r in range(local):
        value = back_ref[r]
        sol_ref[r] = value
        near = near_ref[r]
        for k in range(blocks):
            product = dot_tn(value, near[:, k * width : (k + 1) * width])
            sel_ref[r, k] = (product / count).astype(BF16)
        copy = pltpu.make_async_copy(sel_ref.at[r], sel_hbm.at[r], sems.at[r])
        copy.start()
        copies.append(copy)
    for copy in copies:
        copy.wait()


def solution(mesh):
    n = mesh.shape["rows"]

    def body(probes, factor, inverses, pattern, owner):
        local, count, width = probes.shape
        neighbors = factor.shape[1]
        total = owner.shape[0]
        rows = local * count
        vmem = pl.BlockSpec(memory_space=pltpu.VMEM)
        smem = pl.BlockSpec(memory_space=pltpu.SMEM)
        anywhere = pl.BlockSpec(memory_space=pl.ANY)
        gathered = pltpu.VMEM((n, rows, width), BF16)
        backed, near = pl.pallas_call(
            functools.partial(solve_kernel, n, local, count, neighbors, total),
            out_shape=(
                jax.ShapeDtypeStruct((local, count, width), BF16),
                jax.ShapeDtypeStruct((local, count, (neighbors + 1) * width), BF16),
            ),
            in_specs=[vmem, anywhere, anywhere, smem, smem],
            out_specs=(vmem, vmem),
            scratch_shapes=[
                pltpu.VMEM(factor.shape, BF16),
                pltpu.VMEM(inverses.shape, BF16),
                pltpu.VMEM(factor.shape, BF16),
                pltpu.VMEM(inverses.shape, BF16),
                pltpu.VMEM((local, neighbors + 1, count, width), F32),
                pltpu.SMEM((local, total), jnp.int32),
                gathered,
            ]
            + [gathered] * (3 * ROUNDS)
            + [
                pltpu.SemaphoreType.DMA((2,)),
                pltpu.SemaphoreType.DMA((2 * ROUNDS + 1,)),
                pltpu.SemaphoreType.DMA((2 * ROUNDS + 1,)),
            ],
            compiler_params=pltpu.CompilerParams(
                collective_id=0, has_side_effects=True, vmem_limit_bytes=60 * 1024 * 1024
            ),
            name="solve_rounds",
        )(probes, factor, inverses, pattern.T, owner)
        sol, selected = pl.pallas_call(
            functools.partial(select_kernel, local, count, neighbors + 1),
            out_shape=(
                jax.ShapeDtypeStruct((local, count, width), BF16),
                jax.ShapeDtypeStruct((local, neighbors + 1, width, width), BF16),
            ),
            in_specs=[vmem, vmem],
            out_specs=(vmem, anywhere),
            scratch_shapes=[
                pltpu.VMEM((local, neighbors + 1, width, width), BF16),
                pltpu.SemaphoreType.DMA((local,)),
            ],
            compiler_params=pltpu.CompilerParams(vmem_limit_bytes=60 * 1024 * 1024),
            name="select_blocks",
        )(backed, near)
        return sol, selected

    return jax.shard_map(
        body,
        mesh=mesh,
        in_specs=(
            P("rows", "probes", None),
            P("rows", None, None, None),
            P("rows", None, None),
            P(),
            P(),
        ),
        out_specs=(P("rows", "probes", None), P("rows", "probes", None, None)),
        check_vma=False,
    )
```

```python
import functools

import jax
import jax.numpy as jnp
from jax import lax
from jax.experimental import pallas as pl
from jax.experimental.pallas import tpu as pltpu
from jax.sharding import PartitionSpec as P

LEVELS = 4
ROUNDS = LEVELS - 1
MESH = pl.DeviceIdType.MESH
F32 = jnp.float32
BF16 = jnp.bfloat16


def dot_nt(a, b):
    return lax.dot_general(a, b, (((1,), (1,)), ((), ())), preferred_element_type=F32)


def dot_nn(a, b):
    return lax.dot_general(a, b, (((1,), (0,)), ((), ())), preferred_element_type=F32)


def dot_tn(a, b):
    return lax.dot_general(a, b, (((0,), (0,)), ((), ())), preferred_element_type=F32)


def solve_kernel(n, inner, local, count, neighbors, total, *refs):
    outer = n // inner
    probes_ref, factor_hbm, inv_hbm, pattern_ref, owner_ref = refs[:5]
    back_ref, near_ref = refs[5:7]
    scratch = refs[7:]
    factor_ref, inv_ref, factor_t, inv_t, terms_ref, table_ref, all_probes = scratch[:7]
    ahead = scratch[7 : 7 + ROUNDS]
    outs = scratch[7 + ROUNDS : 7 + 2 * ROUNDS]
    arrive = scratch[7 + 2 * ROUNDS : 7 + 3 * ROUNDS]
    mids = scratch[7 + 3 * ROUNDS : 7 + 4 * ROUNDS]
    finals = scratch[7 + 4 * ROUNDS : 7 + 5 * ROUNDS]
    load_sem, send_sem, recv_sem = scratch[7 + 5 * ROUNDS :]
    unroll = n <= 16
    me = lax.axis_index("rows")
    high = me // inner
    low = me % inner

    load_inv = pltpu.make_async_copy(inv_hbm, inv_ref, load_sem.at[0])
    load_factor = pltpu.make_async_copy(factor_hbm, factor_ref, load_sem.at[1])
    load_inv.start()
    load_factor.start()

    def far(step):
        return lax.rem(high + step, outer)

    def near(step):
        return lax.rem(low + step, inner)

    def copy_to(to, src, dst, at):
        return pltpu.make_async_remote_copy(
            src_ref=src,
            dst_ref=dst,
            send_sem=send_sem.at[at],
            recv_sem=recv_sem.at[at],
            device_id={"rows": to},
            device_id_type=MESH,
        )

    def far_copy(step, src, dst, at):
        return copy_to(far(step) * inner + low, src, dst, at)

    def near_copy(step, src, dst, at):
        return copy_to(high * inner + near(step), src, dst, at)

    def each(steps, one):
        def body(step, carry):
            one(step)
            return carry

        lax.fori_loop(1, steps, body, 0, unroll=unroll)

    barrier = pltpu.get_barrier_semaphore()

    def greet(to):
        pl.semaphore_signal(barrier, inc=1, device_id={"rows": to}, device_id_type=MESH)

    each(outer, lambda step: greet(far(step) * inner + low))
    each(inner, lambda step: greet(high * inner + near(step)))

    def halves(block):
        wide = block.astype(F32)
        return [wide[r * count : (r + 1) * count] for r in range(local)]

    def pick(ref, place, valid):
        parts = halves(ref[place[0], place[1]])
        value = parts[0]
        for r in range(1, local):
            value = jnp.where(place[2] == r, parts[r], value)
        return jnp.where(valid, value, jnp.zeros_like(value)).astype(BF16)

    def all_far(ref, at):
        every = ref.at[0, pl.ds(0, outer - 1)]
        return far_copy(1, every, every, at)

    def all_far_flat(ref, at):
        every = ref.at[pl.ds(0, outer - 1)]
        return far_copy(1, every, every, at)

    def all_near(ref, at):
        every = ref.at[pl.ds(0, inner - 1)]
        return near_copy(1, every, every, at)

    def gather_far(ref, at):
        own = ref.at[low, high]
        each(outer, lambda step: far_copy(step, own, own, at).start())

    def gather_near(ref, at):
        own = ref.at[low]
        each(inner, lambda step: near_copy(step, own, own, at).start())

    probes = [probes_ref[r] for r in range(local)]
    probes_wide = [p.astype(F32) for p in probes]

    load_inv.wait()

    def store_own(ref, values):
        ref[low, high] = jnp.concatenate([v.astype(F32) for v in values], axis=0).astype(BF16)

    solved = [dot_nt(probes[r], inv_ref[r]).astype(BF16) for r in range(local)]
    store_own(ahead[0], solved)
    store_own(all_probes, probes)

    pl.semaphore_wait(barrier, outer + inner - 2)
    gather_far(ahead[0], 0)

    sources, places, valids = [], [], []
    for r in range(local):
        slot = me * local + r
        row = lax.fori_loop(
            0, total, lambda i, found: jnp.where(owner_ref[i] == slot, i, found), 0, unroll=8
        )
        cols = [pattern_ref[k, row] for k in range(neighbors)]
        valids.append([c >= 0 for c in cols])
        slots = [owner_ref[jnp.maximum(c, 0)] for c in cols]
        sources.append(slots)
        places.append(
            [
                (
                    lax.rem(lax.div(s, local), inner),
                    lax.div(s, local * inner),
                    lax.rem(s, local),
                )
                for s in slots
            ]
        )

    all_far(ahead[0], 0).wait_recv()
    gather_near(ahead[0], 1)
    gather_far(all_probes, 4 * ROUNDS)

    def fill(slot, carry):
        for r in range(local):
            found = neighbors
            for k in range(neighbors):
                here = jnp.logical_and(sources[r][k] == slot, valids[r][k])
                found = jnp.where(here, k, found)
            table_ref[r, slot] = found
        return carry

    load_factor.wait()
    for r in range(local):
        for k in range(neighbors):
            factor_t[r, k] = factor_ref[r, k].T

    for level in range(1, LEVELS):
        last = ahead[level - 1]
        if level > 1:
            all_far(last, 2 * level - 2).wait_recv()
            gather_near(last, 2 * level - 1)
        all_near(last, 2 * level - 1).wait_recv()
        resid = []
        for r in range(local):
            total_value = jnp.zeros_like(probes_wide[r])
            for k in range(neighbors):
                value = pick(last, places[r][k], valids[r][k])
                total_value += dot_nn(value, factor_t[r, k])
            resid.append((probes_wide[r] - total_value).astype(BF16))
        solved = [dot_nt(resid[r], inv_ref[r]).astype(BF16) for r in range(local)]
        if level < ROUNDS:
            store_own(ahead[level], solved)
            gather_far(ahead[level], 2 * level)
        if level == 1:
            lax.fori_loop(0, total, fill, 0, unroll=4)
            for r in range(local):
                terms_ref[r, neighbors] = jnp.zeros((count, probes_wide[0].shape[1]), F32)
            all_far(all_probes, 4 * ROUNDS).wait_recv()
            gather_near(all_probes, 4 * ROUNDS + 1)

    solved_wide = [v.astype(F32) for v in solved]
    start = solved
    for turn in range(LEVELS):
        backed = [dot_nn(start[r], inv_ref[r]).astype(BF16) for r in range(local)]
        if turn == ROUNDS:
            break
        for r in range(local):
            for k in range(neighbors):
                terms_ref[r, k] = dot_nn(backed[r], factor_ref[r, k])

        def part(device):
            rows = []
            for q in range(local):
                slot = device * local + q
                value = terms_ref[0, table_ref[0, slot]]
                for r in range(1, local):
                    value += terms_ref[r, table_ref[r, slot]]
                rows.append(value)
            return jnp.concatenate(rows, axis=0)

        out, into, mid, final = outs[turn], arrive[turn], mids[turn], finals[turn]
        at = 2 * (ROUNDS + turn)

        def give(step):
            to = near(step)
            values = [part(z * inner + to).astype(BF16) for z in range(outer)]
            for z in range(outer):
                out[to, z] = values[z]
            near_copy(step, out.at[to], into.at[low], at).start()

        each(inner, give)
        own = [part(z * inner + low) for z in range(outer)]
        for z in range(outer):
            into[low, z] = own[z].astype(BF16)
        all_near(into, at).wait_recv()
        for z in range(outer):
            value = into[0, z].astype(F32)
            for p in range(1, inner):
                value += into[p, z].astype(F32)
            mid[z] = value.astype(BF16)
        each(
            outer,
            lambda step: far_copy(step, mid.at[far(step)], final.at[high], at + 1).start(),
        )
        final[high] = mid[high]
        all_far_flat(final, at + 1).wait_recv()
        acc = final[0].astype(F32)
        for z in range(1, outer):
            acc += final[z].astype(F32)
        start = [
            (solved_wide[r] - acc[r * count : (r + 1) * count]).astype(BF16) for r in range(local)
        ]

    all_near(all_probes, 4 * ROUNDS + 1).wait_recv()
    for r in range(local):
        back_ref[r] = backed[r]
        width = probes_wide[r].shape[1]
        for k in range(neighbors):
            near_ref[r, :, k * width : (k + 1) * width] = pick(
                all_probes, places[r][k], valids[r][k]
            )
        near_ref[r, :, neighbors * width :] = probes[r]

    for level in range(ROUNDS):
        all_far(ahead[level], 2 * level).wait_send()
        all_near(ahead[level], 2 * level + 1).wait_send()
        all_near(outs[level], 2 * (ROUNDS + level)).wait_send()
        all_far_flat(mids[level], 2 * (ROUNDS + level) + 1).wait_send()
    all_far(all_probes, 4 * ROUNDS).wait_send()
    all_near(all_probes, 4 * ROUNDS + 1).wait_send()


def select_kernel(local, count, blocks, back_ref, near_ref, sol_ref, sel_hbm, sel_ref, sems):
    copies = []
    width = back_ref.shape[2]
    for r in range(local):
        value = back_ref[r]
        sol_ref[r] = value
        near = near_ref[r]
        for k in range(blocks):
            product = dot_tn(value, near[:, k * width : (k + 1) * width])
            sel_ref[r, k] = (product / count).astype(BF16)
        copy = pltpu.make_async_copy(sel_ref.at[r], sel_hbm.at[r], sems.at[r])
        copy.start()
        copies.append(copy)
    for copy in copies:
        copy.wait()


def solution(mesh):
    n = mesh.shape["rows"]
    inner = max(d for d in range(1, n + 1) if n % d == 0 and d * d <= n)
    outer = n // inner

    def body(probes, factor, inverses, pattern, owner):
        local, count, width = probes.shape
        neighbors = factor.shape[1]
        total = owner.shape[0]
        rows = local * count
        vmem = pl.BlockSpec(memory_space=pltpu.VMEM)
        smem = pl.BlockSpec(memory_space=pltpu.SMEM)
        anywhere = pl.BlockSpec(memory_space=pl.ANY)
        gathered = pltpu.VMEM((inner, outer, rows, width), BF16)
        column = pltpu.VMEM((outer, rows, width), BF16)
        backed, near = pl.pallas_call(
            functools.partial(solve_kernel, n, inner, local, count, neighbors, total),
            out_shape=(
                jax.ShapeDtypeStruct((local, count, width), BF16),
                jax.ShapeDtypeStruct((local, count, (neighbors + 1) * width), BF16),
            ),
            in_specs=[vmem, anywhere, anywhere, smem, smem],
            out_specs=(vmem, vmem),
            scratch_shapes=[
                pltpu.VMEM(factor.shape, BF16),
                pltpu.VMEM(inverses.shape, BF16),
                pltpu.VMEM(factor.shape, BF16),
                pltpu.VMEM(inverses.shape, BF16),
                pltpu.VMEM((local, neighbors + 1, count, width), F32),
                pltpu.SMEM((local, total), jnp.int32),
                gathered,
            ]
            + [gathered] * (3 * ROUNDS)
            + [column] * (2 * ROUNDS)
            + [
                pltpu.SemaphoreType.DMA((2,)),
                pltpu.SemaphoreType.DMA((4 * ROUNDS + 2,)),
                pltpu.SemaphoreType.DMA((4 * ROUNDS + 2,)),
            ],
            compiler_params=pltpu.CompilerParams(
                collective_id=0, has_side_effects=True, vmem_limit_bytes=65408 * 1024
            ),
            name="solve_rounds",
        )(probes, factor, inverses, pattern.T, owner)
        sol, selected = pl.pallas_call(
            functools.partial(select_kernel, local, count, neighbors + 1),
            out_shape=(
                jax.ShapeDtypeStruct((local, count, width), BF16),
                jax.ShapeDtypeStruct((local, neighbors + 1, width, width), BF16),
            ),
            in_specs=[vmem, vmem],
            out_specs=(vmem, anywhere),
            scratch_shapes=[
                pltpu.VMEM((local, neighbors + 1, width, width), BF16),
                pltpu.SemaphoreType.DMA((local,)),
            ],
            compiler_params=pltpu.CompilerParams(vmem_limit_bytes=16 * 1024 * 1024),
            name="select_blocks",
        )(backed, near)
        return sol, selected

    return jax.shard_map(
        body,
        mesh=mesh,
        in_specs=(
            P("rows", "probes", None),
            P("rows", None, None, None),
            P("rows", None, None),
            P(),
            P(),
        ),
        out_specs=(P("rows", "probes", None), P("rows", "probes", None, None)),
        check_vma=False,
    )
```

```python
import functools

import jax
import jax.numpy as jnp
from jax import lax
from jax.experimental import pallas as pl
from jax.experimental.pallas import tpu as pltpu
from jax.sharding import PartitionSpec as P

LEVELS = 4
ROUNDS = LEVELS - 1
STREAMS = 2
MESH = pl.DeviceIdType.MESH
F32 = jnp.float32
BF16 = jnp.bfloat16


def dot_nt(a, b):
    return lax.dot_general(a, b, (((1,), (1,)), ((), ())), preferred_element_type=F32)


def dot_nn(a, b):
    return lax.dot_general(a, b, (((1,), (0,)), ((), ())), preferred_element_type=F32)


def dot_tn(a, b):
    return lax.dot_general(a, b, (((0,), (0,)), ((), ())), preferred_element_type=F32)


def solve_kernel(n, local, count, neighbors, total, *refs):
    probes_ref, factor_hbm, inv_hbm, pattern_ref, owner_ref = refs[:5]
    back_ref, near_ref = refs[5:7]
    scratch = refs[7:]
    factor_ref, inv_ref, factor_t, inv_t, table_ref, all_probes = scratch[:6]
    terms_refs = scratch[6 : 6 + STREAMS]
    buffers = scratch[6 + STREAMS : 6 + STREAMS * (1 + 3 * ROUNDS)]
    load_sem, send_sem, recv_sem = scratch[6 + STREAMS * (1 + 3 * ROUNDS) :]

    def buffer(kind, turn, s):
        return buffers[(kind * ROUNDS + turn) * STREAMS + s]

    unroll = n <= 16
    group = max(g for g in range(1, 6) if (n - 1) % g == 0)
    width = probes_ref.shape[2]
    half = width // 2
    few = count // STREAMS
    rows = local * few
    probes_at = 2 * ROUNDS * STREAMS
    me = lax.axis_index("rows")

    load_inv = pltpu.make_async_copy(inv_hbm, inv_ref, load_sem.at[0])
    load_factor = pltpu.make_async_copy(factor_hbm, factor_ref, load_sem.at[1])
    load_inv.start()
    load_factor.start()

    def peer(step):
        odd = step % 2
        away = n // 2 + odd * ((step + 1) // 2) - (1 - odd) * (step // 2)
        return lax.rem(me + away, n)

    barrier = pltpu.get_barrier_semaphore()

    def greet(step, carry):
        pl.semaphore_signal(barrier, inc=1, device_id={"rows": peer(step)}, device_id_type=MESH)
        return carry

    lax.fori_loop(0, n - 1, greet, 0, unroll=unroll)

    def fold(value):
        return jnp.concatenate([value[:, :half], value[:, half:]], axis=0).astype(BF16)

    def unfold(block):
        wide = block.astype(F32)
        return jnp.concatenate([wide[:rows], wide[rows:]], axis=1)

    own_row = lax.broadcasted_iota(jnp.int32, (rows, width), 0) // few

    def merge(values):
        result = values[0]
        for r in range(1, local):
            result = jnp.where(own_row == r, values[r], result)
        return result

    def turned(value, places):
        places = places % local
        if places == 0:
            return value
        cut = places * few
        return jnp.concatenate([value[cut:], value[:cut]], axis=0)

    def pick(block, at, r, valid):
        value = turned(block, local - r)
        for q in range(1, local):
            value = jnp.where(at == q, turned(block, q - r + local), value)
        return jnp.where(valid, value, jnp.zeros_like(value)).astype(BF16)

    def pick_probes(slot, valid):
        wide = all_probes[lax.div(slot, local)].astype(F32)
        at = lax.rem(slot, local)
        value = wide[:count]
        for r in range(1, local):
            value = jnp.where(at == r, wide[r * count : (r + 1) * count], value)
        return jnp.where(valid, value, jnp.zeros_like(value)).astype(BF16)

    def send(src, dst, to, at):
        return pltpu.make_async_remote_copy(
            src_ref=src,
            dst_ref=dst.at[me],
            send_sem=send_sem.at[at],
            recv_sem=recv_sem.at[at],
            device_id={"rows": to},
            device_id_type=MESH,
        )

    def whole_of(ref, at):
        every = ref.at[pl.ds(0, n - 1)]
        return pltpu.make_async_remote_copy(
            src_ref=every,
            dst_ref=every,
            send_sem=send_sem.at[at],
            recv_sem=recv_sem.at[at],
            device_id={"rows": peer(0)},
            device_id_type=MESH,
        )

    def broadcast(ref, at, first=0, last=n - 1):
        def one(step, carry):
            send(ref.at[me], ref, peer(step), at).start()
            return carry

        lax.fori_loop(first, last, one, 0, unroll=unroll)

    def share_probes(turn):
        pieces = 2 * ROUNDS - 1
        size = -(-(n - 1) // pieces)
        first = min(turn * size, n - 1)
        last = min(first + size, n - 1)
        if last > first:
            broadcast(all_probes, probes_at, first, last)

    whole = [probes_ref[r].astype(F32) for r in range(local)]
    all_probes[me] = jnp.concatenate(whole, axis=0).astype(BF16)
    probes = [
        jnp.concatenate([w[s * few : (s + 1) * few] for w in whole], axis=0)
        for s in range(STREAMS)
    ]

    load_inv.wait()
    solved = []
    for s in range(STREAMS):
        value = merge([dot_nt(probes[s].astype(BF16), inv_ref[r]) for r in range(local)])
        solved.append(value)
        buffer(0, 0, s)[me] = fold(value)

    pl.semaphore_wait(barrier, n - 1)
    for s in range(STREAMS):
        broadcast(buffer(0, 0, s), s)
    share_probes(0)

    sources, places, valids = [], [], []
    for r in range(local):
        slot = me * local + r
        row = lax.fori_loop(
            0, total, lambda i, found: jnp.where(owner_ref[i] == slot, i, found), 0, unroll=8
        )
        cols = [pattern_ref[k, row] for k in range(neighbors)]
        valids.append([c >= 0 for c in cols])
        slots = [owner_ref[jnp.maximum(c, 0)] for c in cols]
        sources.append(slots)
        places.append([(lax.div(s, local), lax.rem(s, local)) for s in slots])

    def fill(slot, carry):
        for r in range(local):
            found = neighbors
            for k in range(neighbors):
                here = jnp.logical_and(sources[r][k] == slot, valids[r][k])
                found = jnp.where(here, k, found)
            table_ref[r, slot] = found
        return carry

    lax.fori_loop(0, total, fill, 0, unroll=4)
    for s in range(STREAMS):
        for r in range(local):
            terms_refs[s][r, neighbors] = jnp.zeros((rows, width), F32)

    load_factor.wait()
    for r in range(local):
        inv_t[r] = inv_ref[r].T
        for k in range(neighbors):
            factor_t[r, k] = factor_ref[r, k].T

    def step_ahead(level, s):
        last = buffer(0, level - 1, s)
        whole_of(last, (level - 1) * STREAMS + s).wait_recv()
        sums = []
        for r in range(local):
            value = jnp.zeros((rows, width), F32)
            for k in range(neighbors):
                device, at = places[r][k]
                near = pick(unfold(last[device]), at, r, valids[r][k])
                value += dot_nn(near, factor_t[r, k])
            sums.append(value)
        resid = (probes[s] - merge(sums)).astype(BF16)
        solved[s] = merge([dot_nn(resid, inv_t[r]) for r in range(local)])
        if level < ROUNDS:
            ref = buffer(0, level, s)
            ref[me] = fold(solved[s])
            broadcast(ref, level * STREAMS + s)

    backed = [None] * STREAMS

    def step_back(turn, s):
        ended = solved[s].astype(BF16).astype(F32)
        if turn > 0:
            into = buffer(2, turn - 1, s)
            whole_of(into, (ROUNDS + turn - 1) * STREAMS + s).wait_recv()
            acc = into[0].astype(F32)
            for d in range(1, n):
                acc += into[d].astype(F32)
            ended = ended - jnp.concatenate([acc[:rows], acc[rows:]], axis=1)
        start = ended.astype(BF16)
        value = merge([dot_nn(start, inv_ref[r]) for r in range(local)]).astype(BF16)
        backed[s] = value
        if turn == ROUNDS:
            return
        terms_ref = terms_refs[s]
        for r in range(local):
            for k in range(neighbors):
                term = dot_nn(value, factor_ref[r, k])
                terms_ref[r, k] = merge([turned(term, r - q + local) for q in range(local)])

        def part(device):
            values = []
            for q in range(local):
                slot = device * local + q
                found = terms_ref[0, table_ref[0, slot]]
                for r in range(1, local):
                    found += terms_ref[r, table_ref[r, slot]]
                values.append(found)
            return fold(merge(values))

        out, into = buffer(1, turn, s), buffer(2, turn, s)
        at = (ROUNDS + turn) * STREAMS + s

        def some(chunk, carry):
            steps = [chunk * group + i for i in range(group)]
            parts = [part(peer(step)) for step in steps]
            for step, value in zip(steps, parts):
                out[peer(step)] = value
            for step in steps:
                send(out.at[peer(step)], into, peer(step), at).start()
            return carry

        lax.fori_loop(0, (n - 1) // group, some, 0, unroll=unroll)
        into[me] = part(me)

    for level in range(1, LEVELS):
        for s in range(STREAMS):
            step_ahead(level, s)
            if level == ROUNDS:
                step_back(0, s)
        share_probes(level)
    for turn in range(1, LEVELS):
        for s in range(STREAMS):
            step_back(turn, s)
        if turn < ROUNDS - 1:
            share_probes(ROUNDS + turn)

    whole_of(all_probes, probes_at).wait_recv()
    wide = [value.astype(F32) for value in backed]
    for r in range(local):
        back_ref[r] = jnp.concatenate(
            [value[r * few : (r + 1) * few] for value in wide], axis=0
        ).astype(BF16)
        for k in range(neighbors):
            near_ref[r, :, k * width : (k + 1) * width] = pick_probes(sources[r][k], valids[r][k])
        near_ref[r, :, neighbors * width :] = whole[r].astype(BF16)

    for turn in range(ROUNDS):
        for s in range(STREAMS):
            whole_of(buffer(0, turn, s), turn * STREAMS + s).wait_send()
            whole_of(buffer(1, turn, s), (ROUNDS + turn) * STREAMS + s).wait_send()
    whole_of(all_probes, probes_at).wait_send()


def select_kernel(local, count, blocks, back_ref, near_ref, sol_ref, sel_hbm, sel_ref, sems):
    copies = []
    width = back_ref.shape[2]
    for r in range(local):
        value = back_ref[r]
        sol_ref[r] = value
        near = near_ref[r]
        for k in range(blocks):
            product = dot_tn(value, near[:, k * width : (k + 1) * width])
            sel_ref[r, k] = (product / count).astype(BF16)
        copy = pltpu.make_async_copy(sel_ref.at[r], sel_hbm.at[r], sems.at[r])
        copy.start()
        copies.append(copy)
    for copy in copies:
        copy.wait()


def solution(mesh):
    n = mesh.shape["rows"]

    def body(probes, factor, inverses, pattern, owner):
        local, count, width = probes.shape
        neighbors = factor.shape[1]
        total = owner.shape[0]
        rows = local * count
        vmem = pl.BlockSpec(memory_space=pltpu.VMEM)
        smem = pl.BlockSpec(memory_space=pltpu.SMEM)
        anywhere = pl.BlockSpec(memory_space=pl.ANY)
        backed, near = pl.pallas_call(
            functools.partial(solve_kernel, n, local, count, neighbors, total),
            out_shape=(
                jax.ShapeDtypeStruct((local, count, width), BF16),
                jax.ShapeDtypeStruct((local, count, (neighbors + 1) * width), BF16),
            ),
            in_specs=[vmem, anywhere, anywhere, smem, smem],
            out_specs=(vmem, vmem),
            scratch_shapes=[
                pltpu.VMEM(factor.shape, BF16),
                pltpu.VMEM(inverses.shape, BF16),
                pltpu.VMEM(factor.shape, BF16),
                pltpu.VMEM(inverses.shape, BF16),
                pltpu.SMEM((local, total), jnp.int32),
                pltpu.VMEM((n, rows, width), BF16),
            ]
            + [pltpu.VMEM((local, neighbors + 1, rows // STREAMS, width), F32)] * STREAMS
            + [pltpu.VMEM((n, 2 * rows // STREAMS, width // 2), BF16)] * (3 * ROUNDS * STREAMS)
            + [
                pltpu.SemaphoreType.DMA((2,)),
                pltpu.SemaphoreType.DMA((2 * ROUNDS * STREAMS + 1,)),
                pltpu.SemaphoreType.DMA((2 * ROUNDS * STREAMS + 1,)),
            ],
            compiler_params=pltpu.CompilerParams(
                collective_id=0, has_side_effects=True, vmem_limit_bytes=60 * 1024 * 1024
            ),
            name="solve_rounds",
        )(probes, factor, inverses, pattern.T, owner)
        sol, selected = pl.pallas_call(
            functools.partial(select_kernel, local, count, neighbors + 1),
            out_shape=(
                jax.ShapeDtypeStruct((local, count, width), BF16),
                jax.ShapeDtypeStruct((local, neighbors + 1, width, width), BF16),
            ),
            in_specs=[vmem, vmem],
            out_specs=(vmem, anywhere),
            scratch_shapes=[
                pltpu.VMEM((local, neighbors + 1, width, width), BF16),
                pltpu.SemaphoreType.DMA((local,)),
            ],
            compiler_params=pltpu.CompilerParams(vmem_limit_bytes=60 * 1024 * 1024),
            name="select_blocks",
        )(backed, near)
        return sol, selected

    return jax.shard_map(
        body,
        mesh=mesh,
        in_specs=(
            P("rows", "probes", None),
            P("rows", None, None, None),
            P("rows", None, None),
            P(),
            P(),
        ),
        out_specs=(P("rows", "probes", None), P("rows", "probes", None, None)),
        check_vma=False,
    )
```

```python
import functools

import jax
import jax.numpy as jnp
from jax import lax
from jax.experimental import pallas as pl
from jax.experimental.pallas import tpu as pltpu
from jax.sharding import PartitionSpec as P

LEVELS = 4
ROUNDS = LEVELS - 1
STREAMS = 2
MESH = pl.DeviceIdType.MESH
F32 = jnp.float32
BF16 = jnp.bfloat16


def dot_nt(a, b):
    return lax.dot_general(a, b, (((1,), (1,)), ((), ())), preferred_element_type=F32)


def dot_nn(a, b):
    return lax.dot_general(a, b, (((1,), (0,)), ((), ())), preferred_element_type=F32)


def dot_tn(a, b):
    return lax.dot_general(a, b, (((0,), (0,)), ((), ())), preferred_element_type=F32)


def solve_kernel(n, local, count, neighbors, total, *refs):
    probes_ref, factor_hbm, inv_hbm, pattern_ref, owner_ref = refs[:5]
    back_ref, near_ref = refs[5:7]
    scratch = refs[7:]
    factor_ref, inv_ref, factor_t, inv_t, table_ref, all_probes, lent, found_ref, taken = scratch[:9]
    terms_refs = scratch[9 : 9 + STREAMS]
    buffers = scratch[9 + STREAMS : 9 + STREAMS * (1 + 3 * ROUNDS)]
    load_sem, send_sem, recv_sem = scratch[9 + STREAMS * (1 + 3 * ROUNDS) :]

    def buffer(kind, turn, s):
        return buffers[(kind * ROUNDS + turn) * STREAMS + s]

    unroll = n <= 16
    group = max(g for g in range(1, 6) if (n - 1) % g == 0)
    width = probes_ref.shape[2]
    few = count
    rows = local * few
    probes_at = 2 * ROUNDS * STREAMS
    lend_at, return_at = probes_at + 1, probes_at + 2
    me = lax.axis_index("rows")
    core = lax.axis_index("probes")
    leads = core % 2 == 1
    helps = core % 2 == 0
    partner = core + 1 - 2 * (core % 2)

    load_inv = pltpu.make_async_copy(inv_hbm, inv_ref, load_sem.at[0])
    load_factor = pltpu.make_async_copy(factor_hbm, factor_ref, load_sem.at[1])

    @pl.when(leads)
    def _():
        load_inv.start()
        load_factor.start()

    def peer(step):
        odd = step % 2
        away = n // 2 + odd * ((step + 1) // 2) - (1 - odd) * (step // 2)
        return lax.rem(me + away, n)

    barrier = pltpu.get_barrier_semaphore()

    def greet(step, carry):
        pl.semaphore_signal(barrier, inc=1, device_id={"rows": peer(step)}, device_id_type=MESH)
        return carry

    lax.fori_loop(0, n - 1, greet, 0, unroll=unroll)
    pl.semaphore_signal(barrier, inc=1, device_id={"probes": partner}, device_id_type=MESH)

    own_row = lax.broadcasted_iota(jnp.int32, (rows, width), 0) // few

    def merge(values):
        result = values[0]
        for r in range(1, local):
            result = jnp.where(own_row == r, values[r], result)
        return result

    def turned(value, places):
        places = places % local
        if places == 0:
            return value
        cut = places * few
        return jnp.concatenate([value[cut:], value[:cut]], axis=0)

    def pick(block, at, r, valid):
        value = turned(block, local - r)
        for q in range(1, local):
            value = jnp.where(at == q, turned(block, q - r + local), value)
        return jnp.where(valid, value, jnp.zeros_like(value)).astype(BF16)

    def pick_probes(slot, valid):
        wide = all_probes[lax.div(slot, local)].astype(F32)
        at = lax.rem(slot, local)
        value = wide[:count]
        for r in range(1, local):
            value = jnp.where(at == r, wide[r * count : (r + 1) * count], value)
        return jnp.where(valid, value, jnp.zeros_like(value)).astype(BF16)

    def send(src, dst, to, at):
        return pltpu.make_async_remote_copy(
            src_ref=src,
            dst_ref=dst.at[me],
            send_sem=send_sem.at[at],
            recv_sem=recv_sem.at[at],
            device_id={"rows": to},
            device_id_type=MESH,
        )

    def whole_of(ref, at):
        every = ref.at[pl.ds(0, n - 1)]
        return pltpu.make_async_remote_copy(
            src_ref=every,
            dst_ref=every,
            send_sem=send_sem.at[at],
            recv_sem=recv_sem.at[at],
            device_id={"rows": peer(0)},
            device_id_type=MESH,
        )

    def broadcast(ref, at, first=0, last=n - 1):
        def one(step, carry):
            send(ref.at[me], ref, peer(step), at).start()
            return carry

        lax.fori_loop(first, last, one, 0, unroll=unroll)

    def share_probes(turn):
        pieces = 2 * ROUNDS - 1
        size = -(-(n - 1) // pieces)
        first = min(turn * size, n - 1)
        last = min(first + size, n - 1)
        if last > first:
            broadcast(all_probes, probes_at, first, last)

    def pass_on(src, dst, at):
        return pltpu.make_async_remote_copy(
            src_ref=src,
            dst_ref=dst,
            send_sem=send_sem.at[at],
            recv_sem=recv_sem.at[at],
            device_id={"probes": partner},
            device_id_type=MESH,
        )

    lend = pass_on(all_probes.at[me], lent, lend_at)
    give_back = pass_on(found_ref, taken, return_at)
    whole = [probes_ref[r].astype(F32) for r in range(local)]
    stacked = jnp.concatenate(whole, axis=0)
    all_probes[me] = stacked.astype(BF16)

    def begin(s, value):
        ended = merge([dot_nt(value, inv_ref[r]) for r in range(local)])
        buffer(0, 0, s)[me] = ended.astype(BF16)

    @pl.when(leads)
    def _():
        load_inv.wait()
        begin(0, stacked.astype(BF16))

    pl.semaphore_wait(barrier, n)

    @pl.when(helps)
    def _():
        lend.start()
        broadcast(all_probes, probes_at)

    @pl.when(leads)
    def _():
        broadcast(buffer(0, 0, 0), 0)

    sources, places, valids = [], [], []
    for r in range(local):
        slot = me * local + r
        row = lax.fori_loop(
            0, total, lambda i, found: jnp.where(owner_ref[i] == slot, i, found), 0, unroll=8
        )
        cols = [pattern_ref[k, row] for k in range(neighbors)]
        valids.append([c >= 0 for c in cols])
        slots = [owner_ref[jnp.maximum(c, 0)] for c in cols]
        sources.append(slots)
        places.append([(lax.div(s, local), lax.rem(s, local)) for s in slots])

    def fill(slot, carry):
        for r in range(local):
            found = neighbors
            for k in range(neighbors):
                here = jnp.logical_and(sources[r][k] == slot, valids[r][k])
                found = jnp.where(here, k, found)
            table_ref[r, slot] = found
        return carry

    solved = [None] * STREAMS
    backed = [None] * STREAMS

    def step_ahead(level, s):
        last = buffer(0, level - 1, s)
        whole_of(last, (level - 1) * STREAMS + s).wait_recv()
        sums = []
        for r in range(local):
            value = jnp.zeros((rows, width), F32)
            for k in range(neighbors):
                device, at = places[r][k]
                near = pick(last[device].astype(F32), at, r, valids[r][k])
                value += dot_nn(near, factor_t[r, k])
            sums.append(value)
        resid = ((lent if s else all_probes.at[me])[...].astype(F32) - merge(sums)).astype(BF16)
        solved[s] = merge([dot_nn(resid, inv_t[r]) for r in range(local)])
        if level < ROUNDS:
            ref = buffer(0, level, s)
            ref[me] = solved[s].astype(BF16)
            broadcast(ref, level * STREAMS + s)

    def step_back(turn, s):
        ended = solved[s].astype(BF16).astype(F32)
        if turn > 0:
            into = buffer(2, turn - 1, s)
            whole_of(into, (ROUNDS + turn - 1) * STREAMS + s).wait_recv()
            acc = into[0].astype(F32)
            for d in range(1, n):
                acc += into[d].astype(F32)
            ended = ended - acc
        start = ended.astype(BF16)
        value = merge([dot_nn(start, inv_ref[r]) for r in range(local)]).astype(BF16)
        backed[s] = value
        if turn == ROUNDS:
            return
        terms_ref = terms_refs[s]
        for r in range(local):
            for k in range(neighbors):
                term = dot_nn(value, factor_ref[r, k])
                terms_ref[r, k] = merge([turned(term, r - q + local) for q in range(local)])

        def part(device):
            values = []
            for q in range(local):
                slot = device * local + q
                found = terms_ref[0, table_ref[0, slot]]
                for r in range(1, local):
                    found += terms_ref[r, table_ref[r, slot]]
                values.append(found)
            return merge(values).astype(BF16)

        out, into = buffer(1, turn, s), buffer(2, turn, s)
        at = (ROUNDS + turn) * STREAMS + s

        def some(chunk, carry):
            steps = [chunk * group + i for i in range(group)]
            parts = [part(peer(step)) for step in steps]
            for step, value in zip(steps, parts):
                out[peer(step)] = value
            for step in steps:
                send(out.at[peer(step)], into, peer(step), at).start()
            return carry

        lax.fori_loop(0, (n - 1) // group, some, 0, unroll=unroll)
        into[me] = part(me)

    @pl.when(leads)
    def _():
        lend.wait_recv()
        begin(1, lent[...])
        broadcast(buffer(0, 0, 1), 1)
        share_probes(0)
        lax.fori_loop(0, total, fill, 0, unroll=4)
        for s in range(STREAMS):
            for r in range(local):
                terms_refs[s][r, neighbors] = jnp.zeros((rows, width), F32)
        load_factor.wait()
        for r in range(local):
            inv_t[r] = inv_ref[r].T
            for k in range(neighbors):
                factor_t[r, k] = factor_ref[r, k].T
        for level in range(1, LEVELS):
            for s in range(STREAMS):
                step_ahead(level, s)
                if level == ROUNDS:
                    step_back(0, s)
            share_probes(level)
        for turn in range(1, LEVELS):
            for s in range(STREAMS):
                step_back(turn, s)
            if turn < ROUNDS - 1:
                share_probes(ROUNDS + turn)
        found_ref[...] = backed[1]
        give_back.start()
        value = backed[0].astype(F32)
        for r in range(local):
            back_ref[r] = value[r * few : (r + 1) * few].astype(BF16)

    whole_of(all_probes, probes_at).wait_recv()
    for r in range(local):
        for k in range(neighbors):
            near_ref[r, :, k * width : (k + 1) * width] = pick_probes(sources[r][k], valids[r][k])
        near_ref[r, :, neighbors * width :] = whole[r].astype(BF16)

    @pl.when(leads)
    def _():
        for turn in range(ROUNDS):
            for s in range(STREAMS):
                whole_of(buffer(0, turn, s), turn * STREAMS + s).wait_send()
                whole_of(buffer(1, turn, s), (ROUNDS + turn) * STREAMS + s).wait_send()
        give_back.wait_send()

    @pl.when(helps)
    def _():
        give_back.wait_recv()
        value = taken[...].astype(F32)
        for r in range(local):
            back_ref[r] = value[r * few : (r + 1) * few].astype(BF16)
        lend.wait_send()

    whole_of(all_probes, probes_at).wait_send()


def select_kernel(local, count, blocks, back_ref, near_ref, sol_ref, sel_hbm, sel_ref, sems):
    copies = []
    width = back_ref.shape[2]
    for r in range(local):
        value = back_ref[r]
        sol_ref[r] = value
        near = near_ref[r]
        for k in range(blocks):
            product = dot_tn(value, near[:, k * width : (k + 1) * width])
            sel_ref[r, k] = (product / count).astype(BF16)
        copy = pltpu.make_async_copy(sel_ref.at[r], sel_hbm.at[r], sems.at[r])
        copy.start()
        copies.append(copy)
    for copy in copies:
        copy.wait()


def solution(mesh):
    n = mesh.shape["rows"]

    def body(probes, factor, inverses, pattern, owner):
        local, count, width = probes.shape
        neighbors = factor.shape[1]
        total = owner.shape[0]
        rows = local * count
        vmem = pl.BlockSpec(memory_space=pltpu.VMEM)
        smem = pl.BlockSpec(memory_space=pltpu.SMEM)
        anywhere = pl.BlockSpec(memory_space=pl.ANY)
        backed, near = pl.pallas_call(
            functools.partial(solve_kernel, n, local, count, neighbors, total),
            out_shape=(
                jax.ShapeDtypeStruct((local, count, width), BF16),
                jax.ShapeDtypeStruct((local, count, (neighbors + 1) * width), BF16),
            ),
            in_specs=[vmem, anywhere, anywhere, smem, smem],
            out_specs=(vmem, vmem),
            scratch_shapes=[
                pltpu.VMEM(factor.shape, BF16),
                pltpu.VMEM(inverses.shape, BF16),
                pltpu.VMEM(factor.shape, BF16),
                pltpu.VMEM(inverses.shape, BF16),
                pltpu.SMEM((local, total), jnp.int32),
                pltpu.VMEM((n, rows, width), BF16),
                pltpu.VMEM((rows, width), BF16),
                pltpu.VMEM((rows, width), BF16),
                pltpu.VMEM((rows, width), BF16),
            ]
            + [pltpu.VMEM((local, neighbors + 1, rows, width), F32)] * STREAMS
            + [pltpu.VMEM((n, rows, width), BF16)] * (3 * ROUNDS * STREAMS)
            + [
                pltpu.SemaphoreType.DMA((2,)),
                pltpu.SemaphoreType.DMA((2 * ROUNDS * STREAMS + 3,)),
                pltpu.SemaphoreType.DMA((2 * ROUNDS * STREAMS + 3,)),
            ],
            compiler_params=pltpu.CompilerParams(
                collective_id=0, has_side_effects=True, vmem_limit_bytes=60 * 1024 * 1024
            ),
            name="solve_rounds",
        )(probes, factor, inverses, pattern.T, owner)
        sol, selected = pl.pallas_call(
            functools.partial(select_kernel, local, count, neighbors + 1),
            out_shape=(
                jax.ShapeDtypeStruct((local, count, width), BF16),
                jax.ShapeDtypeStruct((local, neighbors + 1, width, width), BF16),
            ),
            in_specs=[vmem, vmem],
            out_specs=(vmem, anywhere),
            scratch_shapes=[
                pltpu.VMEM((local, neighbors + 1, width, width), BF16),
                pltpu.SemaphoreType.DMA((local,)),
            ],
            compiler_params=pltpu.CompilerParams(vmem_limit_bytes=60 * 1024 * 1024),
            name="select_blocks",
        )(backed, near)
        return sol, selected

    return jax.shard_map(
        body,
        mesh=mesh,
        in_specs=(
            P("rows", "probes", None),
            P("rows", None, None, None),
            P("rows", None, None),
            P(),
            P(),
        ),
        out_specs=(P("rows", "probes", None), P("rows", "probes", None, None)),
        check_vma=False,
    )
```

```python
import functools

import jax
import jax.numpy as jnp
from jax import lax
from jax.experimental import pallas as pl
from jax.experimental.pallas import tpu as pltpu
from jax.sharding import PartitionSpec as P

LEVELS = 4
ROUNDS = LEVELS - 1
STREAMS = 2
MESH = pl.DeviceIdType.MESH
F32 = jnp.float32
BF16 = jnp.bfloat16


def dot_nt(a, b):
    return lax.dot_general(a, b, (((1,), (1,)), ((), ())), preferred_element_type=F32)


def dot_nn(a, b):
    return lax.dot_general(a, b, (((1,), (0,)), ((), ())), preferred_element_type=F32)


def dot_tn(a, b):
    return lax.dot_general(a, b, (((0,), (0,)), ((), ())), preferred_element_type=F32)


def solve_kernel(n, inner, local, count, neighbors, total, *refs):
    probes_hbm, factor_hbm, inv_hbm, pattern_hbm, owner_hbm = refs[:5]
    back_ref, near_ref = refs[5:7]
    scratch = refs[7:]
    factor_ref, inv_ref, factor_t, inv_t, table_ref, probes_ref, pattern_ref, owner_ref = scratch[:8]
    pairs, own_probes, lent, found_ref, taken, near_out, near_in = scratch[8:15]
    terms_refs = scratch[15 : 15 + STREAMS]
    buffers = scratch[15 + STREAMS : 15 + STREAMS * (1 + 3 * ROUNDS)]
    load_sem, send_sem, recv_sem = scratch[15 + STREAMS * (1 + 3 * ROUNDS) :]
    outer = n // inner

    def buffer(kind, turn, s):
        return buffers[(kind * ROUNDS + turn) * STREAMS + s]

    unroll = n <= 16
    group = max(g for g in range(1, 6) if (n - 1) % g == 0)
    width = probes_ref.shape[2]
    few = count
    rows = local * few
    probes_at = 2 * ROUNDS * STREAMS
    lend_at, return_at, near_at = probes_at + 2, probes_at + 3, probes_at + 4
    me = lax.axis_index("rows")
    core = lax.axis_index("probes")
    leads = core % 2 == 1
    helps = core % 2 == 0
    partner = core + 1 - 2 * (core % 2)

    load_inv = pltpu.make_async_copy(inv_hbm, inv_ref, load_sem.at[0])
    load_factor = pltpu.make_async_copy(factor_hbm, factor_ref, load_sem.at[1])
    load_probes = pltpu.make_async_copy(probes_hbm, probes_ref, load_sem.at[2])
    load_pattern = pltpu.make_async_copy(pattern_hbm, pattern_ref, load_sem.at[3])
    load_owner = pltpu.make_async_copy(owner_hbm, owner_ref, load_sem.at[4])
    load_probes.start()

    @pl.when(leads)
    def _():
        load_inv.start()

    load_pattern.start()
    load_owner.start()

    @pl.when(leads)
    def _():
        load_factor.start()

    def peer(step):
        odd = step % 2
        away = n // 2 + odd * ((step + 1) // 2) - (1 - odd) * (step // 2)
        return lax.rem(me + away, n)

    barrier = pltpu.get_barrier_semaphore()

    def greet(step, carry):
        pl.semaphore_signal(barrier, inc=1, device_id={"rows": peer(step)}, device_id_type=MESH)
        return carry

    lax.fori_loop(0, n - 1, greet, 0, unroll=unroll)
    pl.semaphore_signal(barrier, inc=1, device_id={"probes": partner}, device_id_type=MESH)

    own_row = lax.broadcasted_iota(jnp.int32, (rows, width), 0) // few

    def merge(values):
        result = values[0]
        for r in range(1, local):
            result = jnp.where(own_row == r, values[r], result)
        return result

    def turned(value, places):
        places = places % local
        if places == 0:
            return value
        cut = places * few
        return jnp.concatenate([value[cut:], value[:cut]], axis=0)

    def pick(block, at, r, valid):
        value = turned(block, local - r)
        for q in range(1, local):
            value = jnp.where(at == q, turned(block, q - r + local), value)
        return jnp.where(valid, value, jnp.zeros_like(value)).astype(BF16)

    def pick_pair(slot, valid, first):
        device = lax.div(slot, local)
        block = pairs[lax.rem(device, inner), lax.div(device, inner)].astype(F32)
        at = lax.rem(slot, local)
        value = block[first : first + count]
        for r in range(1, local):
            low_row = first + r * count
            value = jnp.where(at == r, block[low_row : low_row + count], value)
        return jnp.where(valid, value, jnp.zeros_like(value)).astype(BF16)

    def send(src, dst, to, at):
        return pltpu.make_async_remote_copy(
            src_ref=src,
            dst_ref=dst.at[me],
            send_sem=send_sem.at[at],
            recv_sem=recv_sem.at[at],
            device_id={"rows": to},
            device_id_type=MESH,
        )

    def whole_of(ref, at):
        every = ref.at[pl.ds(0, n - 1)]
        return pltpu.make_async_remote_copy(
            src_ref=every,
            dst_ref=every,
            send_sem=send_sem.at[at],
            recv_sem=recv_sem.at[at],
            device_id={"rows": peer(0)},
            device_id_type=MESH,
        )

    def broadcast(ref, at, first=0, last=n - 1):
        def one(step, carry):
            send(ref.at[me], ref, peer(step), at).start()
            return carry

        lax.fori_loop(first, last, one, 0, unroll=unroll)

    def pass_on(src, dst, at):
        return pltpu.make_async_remote_copy(
            src_ref=src,
            dst_ref=dst,
            send_sem=send_sem.at[at],
            recv_sem=recv_sem.at[at],
            device_id={"probes": partner},
            device_id_type=MESH,
        )

    lend = pass_on(own_probes, lent, lend_at)
    give_back = pass_on(found_ref, taken, return_at)
    give_near = pass_on(near_out, near_in, near_at)
    load_probes.wait()
    whole = [probes_ref[r].astype(F32) for r in range(local)]
    stacked = jnp.concatenate(whole, axis=0)
    own_probes[...] = stacked.astype(BF16)

    def begin(s, value):
        ended = merge([dot_nt(value, inv_ref[r]) for r in range(local)])
        buffer(0, 0, s)[me] = ended.astype(BF16)

    @pl.when(leads)
    def _():
        load_inv.wait()
        begin(0, stacked.astype(BF16))

    pl.semaphore_wait(barrier, n)

    lend.start()

    @pl.when(leads)
    def _():
        broadcast(buffer(0, 0, 0), 0)

    load_pattern.wait()
    load_owner.wait()

    sources, places, valids = [], [], []
    for r in range(local):
        slot = me * local + r
        row = lax.fori_loop(
            0, total, lambda i, found: jnp.where(owner_ref[i] == slot, i, found), 0, unroll=8
        )
        cols = [pattern_ref[k, row] for k in range(neighbors)]
        valids.append([c >= 0 for c in cols])
        slots = [owner_ref[jnp.maximum(c, 0)] for c in cols]
        sources.append(slots)
        places.append([(lax.div(s, local), lax.rem(s, local)) for s in slots])

    def fill(slot, carry):
        for r in range(local):
            found = neighbors
            for k in range(neighbors):
                here = jnp.logical_and(sources[r][k] == slot, valids[r][k])
                found = jnp.where(here, k, found)
            table_ref[r, slot] = found
        return carry

    solved = [None] * STREAMS
    backed = [None] * STREAMS

    def step_ahead(level, s):
        last = buffer(0, level - 1, s)
        whole_of(last, (level - 1) * STREAMS + s).wait_recv()
        sums = []
        for r in range(local):
            value = jnp.zeros((rows, width), F32)
            for k in range(neighbors):
                device, at = places[r][k]
                near = pick(last[device].astype(F32), at, r, valids[r][k])
                value += dot_nn(near, factor_t[r, k])
            sums.append(value)
        resid = ((lent if s else own_probes)[...].astype(F32) - merge(sums)).astype(BF16)
        solved[s] = merge([dot_nn(resid, inv_t[r]) for r in range(local)])
        if level < ROUNDS:
            ref = buffer(0, level, s)
            ref[me] = solved[s].astype(BF16)
            broadcast(ref, level * STREAMS + s)

    def step_back(turn, s):
        ended = solved[s].astype(BF16).astype(F32)
        if turn > 0:
            into = buffer(2, turn - 1, s)
            whole_of(into, (ROUNDS + turn - 1) * STREAMS + s).wait_recv()
            acc = into[0].astype(F32)
            for d in range(1, n):
                acc += into[d].astype(F32)
            ended = ended - acc
        start = ended.astype(BF16)
        value = merge([dot_nn(start, inv_ref[r]) for r in range(local)]).astype(BF16)
        backed[s] = value
        if turn == ROUNDS:
            return
        terms_ref = terms_refs[s]
        for r in range(local):
            for k in range(neighbors):
                term = dot_nn(value, factor_ref[r, k])
                terms_ref[r, k] = merge([turned(term, r - q + local) for q in range(local)])

        def part(device):
            values = []
            for q in range(local):
                slot = device * local + q
                found = terms_ref[0, table_ref[0, slot]]
                for r in range(1, local):
                    found += terms_ref[r, table_ref[r, slot]]
                values.append(found)
            return merge(values).astype(BF16)

        out, into = buffer(1, turn, s), buffer(2, turn, s)
        at = (ROUNDS + turn) * STREAMS + s

        def some(chunk, carry):
            steps = [chunk * group + i for i in range(group)]
            parts = [part(peer(step)) for step in steps]
            for step, value in zip(steps, parts):
                out[peer(step)] = value
            for step in steps:
                send(out.at[peer(step)], into, peer(step), at).start()
            return carry

        lax.fori_loop(0, (n - 1) // group, some, 0, unroll=unroll)
        into[me] = part(me)

    @pl.when(leads)
    def _():
        lend.wait_recv()
        begin(1, lent[...])
        broadcast(buffer(0, 0, 1), 1)
        lax.fori_loop(0, total, fill, 0, unroll=4)
        for s in range(STREAMS):
            for r in range(local):
                terms_refs[s][r, neighbors] = jnp.zeros((rows, width), F32)
        load_factor.wait()
        for r in range(local):
            inv_t[r] = inv_ref[r].T
            for k in range(neighbors):
                factor_t[r, k] = factor_ref[r, k].T
        for level in range(1, LEVELS):
            for s in range(STREAMS):
                step_ahead(level, s)
                if level == ROUNDS:
                    step_back(0, s)
        for turn in range(1, LEVELS):
            for s in range(STREAMS):
                step_back(turn, s)
        found_ref[...] = backed[1]
        give_back.start()
        value = backed[0].astype(F32)
        for r in range(local):
            back_ref[r] = value[r * few : (r + 1) * few].astype(BF16)

        give_near.wait_recv()
        handed = near_in[...].astype(F32)
        for r in range(local):
            near_ref[r, :, : neighbors * width] = handed[r * count : (r + 1) * count].astype(BF16)
        for turn in range(ROUNDS):
            for s in range(STREAMS):
                whole_of(buffer(0, turn, s), turn * STREAMS + s).wait_send()
                whole_of(buffer(1, turn, s), (ROUNDS + turn) * STREAMS + s).wait_send()
        give_back.wait_send()

    @pl.when(helps)
    def _():
        high, low = me // inner, me % inner
        lend.wait_recv()
        pairs[low, high] = jnp.concatenate([stacked, lent[...].astype(F32)], axis=0).astype(BF16)

        def to_far(step, src):
            to = lax.rem(high + step, outer) * inner + low
            return pltpu.make_async_remote_copy(
                src_ref=src,
                dst_ref=src,
                send_sem=send_sem.at[probes_at],
                recv_sem=recv_sem.at[probes_at],
                device_id={"rows": to},
                device_id_type=MESH,
            )

        def to_near(step, src):
            to = high * inner + lax.rem(low + step, inner)
            return pltpu.make_async_remote_copy(
                src_ref=src,
                dst_ref=src,
                send_sem=send_sem.at[probes_at + 1],
                recv_sem=recv_sem.at[probes_at + 1],
                device_id={"rows": to},
                device_id_type=MESH,
            )

        for step in range(1, outer):
            to_far(step, pairs.at[low, high]).start()
        far_all = to_far(1, pairs.at[0, pl.ds(0, outer - 1)])
        far_all.wait_recv()
        for step in range(1, inner):
            to_near(step, pairs.at[low]).start()
        near_all = to_near(1, pairs.at[pl.ds(0, inner - 1)])
        near_all.wait_recv()
        for k in range(neighbors):
            span = slice(k * width, (k + 1) * width)
            theirs = []
            for r in range(local):
                near_ref[r, :, span] = pick_pair(sources[r][k], valids[r][k], 0)
                theirs.append(pick_pair(sources[r][k], valids[r][k], rows).astype(F32))
            near_out[:, span] = jnp.concatenate(theirs, axis=0).astype(BF16)
        give_near.start()
        far_all.wait_send()
        near_all.wait_send()
        give_back.wait_recv()
        value = taken[...].astype(F32)
        for r in range(local):
            back_ref[r] = value[r * few : (r + 1) * few].astype(BF16)
        give_near.wait_send()

    for r in range(local):
        near_ref[r, :, neighbors * width :] = whole[r].astype(BF16)
    lend.wait_send()


def select_kernel(local, count, blocks, back_ref, near_ref, sol_ref, sel_hbm, sel_ref, sems):
    copies = []
    width = back_ref.shape[2]
    for r in range(local):
        value = back_ref[r]
        sol_ref[r] = value
        near = near_ref[r]
        for k in range(blocks):
            product = dot_tn(value, near[:, k * width : (k + 1) * width])
            sel_ref[r, k] = (product / count).astype(BF16)
        copy = pltpu.make_async_copy(sel_ref.at[r], sel_hbm.at[r], sems.at[r])
        copy.start()
        copies.append(copy)
    for copy in copies:
        copy.wait()


def solution(mesh):
    n = mesh.shape["rows"]
    inner = max(d for d in range(1, n + 1) if n % d == 0 and d * d <= n)

    def body(probes, factor, inverses, pattern, owner):
        local, count, width = probes.shape
        neighbors = factor.shape[1]
        total = owner.shape[0]
        rows = local * count
        vmem = pl.BlockSpec(memory_space=pltpu.VMEM)
        anywhere = pl.BlockSpec(memory_space=pl.ANY)
        backed, near = pl.pallas_call(
            functools.partial(solve_kernel, n, inner, local, count, neighbors, total),
            out_shape=(
                jax.ShapeDtypeStruct((local, count, width), BF16),
                jax.ShapeDtypeStruct((local, count, (neighbors + 1) * width), BF16),
            ),
            in_specs=[pl.BlockSpec(memory_space=pltpu.HBM)] * 5,
            out_specs=(vmem, vmem),
            scratch_shapes=[
                pltpu.VMEM(factor.shape, BF16),
                pltpu.VMEM(inverses.shape, BF16),
                pltpu.VMEM(factor.shape, BF16),
                pltpu.VMEM(inverses.shape, BF16),
                pltpu.SMEM((local, total), jnp.int32),
                pltpu.VMEM(probes.shape, BF16),
                pltpu.SMEM((neighbors, total), jnp.int32),
                pltpu.SMEM((total,), jnp.int32),
                pltpu.VMEM((inner, n // inner, 2 * rows, width), BF16),
            ]
            + [pltpu.VMEM((rows, width), BF16)] * 4
            + [pltpu.VMEM((rows, neighbors * width), BF16)] * 2
            + [pltpu.VMEM((local, neighbors + 1, rows, width), F32)] * STREAMS
            + [pltpu.VMEM((n, rows, width), BF16)] * (3 * ROUNDS * STREAMS)
            + [
                pltpu.SemaphoreType.DMA((5,)),
                pltpu.SemaphoreType.DMA((2 * ROUNDS * STREAMS + 5,)),
                pltpu.SemaphoreType.DMA((2 * ROUNDS * STREAMS + 5,)),
            ],
            compiler_params=pltpu.CompilerParams(
                collective_id=0, has_side_effects=True, vmem_limit_bytes=60 * 1024 * 1024
            ),
            name="solve_rounds",
        )(probes, factor, inverses, pattern.T, owner)
        sol, selected = pl.pallas_call(
            functools.partial(select_kernel, local, count, neighbors + 1),
            out_shape=(
                jax.ShapeDtypeStruct((local, count, width), BF16),
                jax.ShapeDtypeStruct((local, neighbors + 1, width, width), BF16),
            ),
            in_specs=[vmem, vmem],
            out_specs=(vmem, anywhere),
            scratch_shapes=[
                pltpu.VMEM((local, neighbors + 1, width, width), BF16),
                pltpu.SemaphoreType.DMA((local,)),
            ],
            compiler_params=pltpu.CompilerParams(vmem_limit_bytes=60 * 1024 * 1024),
            name="select_blocks",
        )(backed, near)
        return sol, selected

    return jax.shard_map(
        body,
        mesh=mesh,
        in_specs=(
            P("rows", "probes", None),
            P("rows", None, None, None),
            P("rows", None, None),
            P(),
            P(),
        ),
        out_specs=(P("rows", "probes", None), P("rows", "probes", None, None)),
        check_vma=False,
    )
```

```python
import functools

import jax
import jax.numpy as jnp
from jax import lax
from jax.experimental import pallas as pl
from jax.experimental.pallas import tpu as pltpu
from jax.sharding import PartitionSpec as P

LEVELS = 4
ROUNDS = LEVELS - 1
STREAMS = 2
MESH = pl.DeviceIdType.MESH
F32 = jnp.float32
BF16 = jnp.bfloat16


def dot_nt(a, b):
    return lax.dot_general(a, b, (((1,), (1,)), ((), ())), preferred_element_type=F32)


def dot_nn(a, b):
    return lax.dot_general(a, b, (((1,), (0,)), ((), ())), preferred_element_type=F32)


def dot_tn(a, b):
    return lax.dot_general(a, b, (((0,), (0,)), ((), ())), preferred_element_type=F32)


def solve_kernel(n, inner, local, count, neighbors, total, *refs):
    probes_hbm, factor_hbm, inv_hbm, pattern_hbm, owner_hbm = refs[:5]
    back_ref, near_ref = refs[5:7]
    scratch = refs[7:]
    factor_ref, inv_ref, table_ref, probes_ref, pattern_ref, owner_ref = scratch[:6]
    pairs, own_probes, lent, found_ref, taken, near_out, near_in = scratch[6:13]
    terms_refs = scratch[13 : 13 + STREAMS]
    buffers = scratch[13 + STREAMS : 13 + STREAMS * (1 + 3 * ROUNDS)]
    load_sem, send_sem, recv_sem = scratch[13 + STREAMS * (1 + 3 * ROUNDS) :]
    outer = n // inner

    def buffer(kind, turn, s):
        return buffers[(kind * ROUNDS + turn) * STREAMS + s]

    unroll = n <= 16
    group = max(g for g in range(1, 6) if (n - 1) % g == 0)
    width = probes_ref.shape[2]
    few = count
    rows = local * few
    probes_at = 2 * ROUNDS * STREAMS
    lend_at, return_at, near_at = probes_at + 2, probes_at + 3, probes_at + 4
    me = lax.axis_index("rows")
    core = lax.axis_index("probes")
    leads = core % 2 == 1
    helps = core % 2 == 0
    partner = core + 1 - 2 * (core % 2)

    load_inv = pltpu.make_async_copy(inv_hbm, inv_ref, load_sem.at[0])
    load_factor = pltpu.make_async_copy(factor_hbm, factor_ref, load_sem.at[1])
    load_probes = pltpu.make_async_copy(probes_hbm, probes_ref, load_sem.at[2])
    load_pattern = pltpu.make_async_copy(pattern_hbm, pattern_ref, load_sem.at[3])
    load_owner = pltpu.make_async_copy(owner_hbm, owner_ref, load_sem.at[4])
    load_probes.start()

    @pl.when(leads)
    def _():
        load_inv.start()

    load_pattern.start()
    load_owner.start()

    @pl.when(leads)
    def _():
        load_factor.start()

    def peer(step):
        odd = step % 2
        away = n // 2 + odd * ((step + 1) // 2) - (1 - odd) * (step // 2)
        return lax.rem(me + away, n)

    barrier = pltpu.get_barrier_semaphore()

    def greet(step, carry):
        pl.semaphore_signal(barrier, inc=1, device_id={"rows": peer(step)}, device_id_type=MESH)
        return carry

    lax.fori_loop(0, n - 1, greet, 0, unroll=unroll)
    pl.semaphore_signal(barrier, inc=1, device_id={"probes": partner}, device_id_type=MESH)

    own_row = lax.broadcasted_iota(jnp.int32, (rows, width), 0) // few

    def merge(values):
        result = values[0]
        for r in range(1, local):
            result = jnp.where(own_row == r, values[r], result)
        return result

    def turned(value, places):
        places = places % local
        if places == 0:
            return value
        cut = places * few
        return jnp.concatenate([value[cut:], value[:cut]], axis=0)

    def pick(block, at, r, valid):
        value = turned(block, local - r)
        for q in range(1, local):
            value = jnp.where(at == q, turned(block, q - r + local), value)
        return jnp.where(valid, value, jnp.zeros_like(value)).astype(BF16)

    def pick_pair(slot, valid, first):
        device = lax.div(slot, local)
        block = pairs[lax.rem(device, inner), lax.div(device, inner)].astype(F32)
        at = lax.rem(slot, local)
        value = block[first : first + count]
        for r in range(1, local):
            low_row = first + r * count
            value = jnp.where(at == r, block[low_row : low_row + count], value)
        return jnp.where(valid, value, jnp.zeros_like(value)).astype(BF16)

    def send(src, dst, to, at):
        return pltpu.make_async_remote_copy(
            src_ref=src,
            dst_ref=dst.at[me],
            send_sem=send_sem.at[at],
            recv_sem=recv_sem.at[at],
            device_id={"rows": to},
            device_id_type=MESH,
        )

    def whole_of(ref, at):
        every = ref.at[pl.ds(0, n - 1)]
        return pltpu.make_async_remote_copy(
            src_ref=every,
            dst_ref=every,
            send_sem=send_sem.at[at],
            recv_sem=recv_sem.at[at],
            device_id={"rows": peer(0)},
            device_id_type=MESH,
        )

    def broadcast(ref, at, first=0, last=n - 1):
        def one(step, carry):
            send(ref.at[me], ref, peer(step), at).start()
            return carry

        lax.fori_loop(first, last, one, 0, unroll=unroll)

    def pass_on(src, dst, at):
        return pltpu.make_async_remote_copy(
            src_ref=src,
            dst_ref=dst,
            send_sem=send_sem.at[at],
            recv_sem=recv_sem.at[at],
            device_id={"probes": partner},
            device_id_type=MESH,
        )

    lend = pass_on(own_probes, lent, lend_at)
    give_back = pass_on(found_ref, taken, return_at)
    give_near = pass_on(near_out, near_in, near_at)
    load_probes.wait()
    whole = [probes_ref[r].astype(F32) for r in range(local)]
    stacked = jnp.concatenate(whole, axis=0)
    own_probes[...] = stacked.astype(BF16)

    def begin(s, value):
        ended = merge([dot_nt(value, inv_ref[r]) for r in range(local)])
        buffer(0, 0, s)[me] = ended.astype(BF16)

    @pl.when(leads)
    def _():
        load_inv.wait()
        begin(0, stacked.astype(BF16))

    pl.semaphore_wait(barrier, n)

    lend.start()

    @pl.when(leads)
    def _():
        broadcast(buffer(0, 0, 0), 0)

    load_pattern.wait()
    load_owner.wait()

    sources, places, valids = [], [], []
    for r in range(local):
        slot = me * local + r
        row = lax.fori_loop(
            0, total, lambda i, found: jnp.where(owner_ref[i] == slot, i, found), 0, unroll=8
        )
        cols = [pattern_ref[k, row] for k in range(neighbors)]
        valids.append([c >= 0 for c in cols])
        slots = [owner_ref[jnp.maximum(c, 0)] for c in cols]
        sources.append(slots)
        places.append([(lax.div(s, local), lax.rem(s, local)) for s in slots])

    def fill(slot, carry):
        for r in range(local):
            found = neighbors
            for k in range(neighbors):
                here = jnp.logical_and(sources[r][k] == slot, valids[r][k])
                found = jnp.where(here, k, found)
            table_ref[r, slot] = found
        return carry

    solved = [None] * STREAMS
    backed = [None] * STREAMS

    def step_ahead(level, s):
        last = buffer(0, level - 1, s)
        whole_of(last, (level - 1) * STREAMS + s).wait_recv()
        sums = []
        for r in range(local):
            value = jnp.zeros((rows, width), F32)
            for k in range(neighbors):
                device, at = places[r][k]
                near = pick(last[device].astype(F32), at, r, valids[r][k])
                value += dot_nt(near, factor_ref[r, k])
            sums.append(value)
        resid = ((lent if s else own_probes)[...].astype(F32) - merge(sums)).astype(BF16)
        solved[s] = merge([dot_nt(resid, inv_ref[r]) for r in range(local)])
        if level < ROUNDS:
            ref = buffer(0, level, s)
            ref[me] = solved[s].astype(BF16)
            broadcast(ref, level * STREAMS + s)

    def step_back(turn, s):
        ended = solved[s].astype(BF16).astype(F32)
        if turn > 0:
            into = buffer(2, turn - 1, s)
            whole_of(into, (ROUNDS + turn - 1) * STREAMS + s).wait_recv()
            acc = into[0].astype(F32)
            for d in range(1, n):
                acc += into[d].astype(F32)
            ended = ended - acc
        start = ended.astype(BF16)
        value = merge([dot_nn(start, inv_ref[r]) for r in range(local)]).astype(BF16)
        backed[s] = value
        if turn == ROUNDS:
            return
        terms_ref = terms_refs[s]
        for r in range(local):
            for k in range(neighbors):
                term = dot_nn(value, factor_ref[r, k])
                terms_ref[r, k] = merge([turned(term, r - q + local) for q in range(local)])

        def part(device):
            values = []
            for q in range(local):
                slot = device * local + q
                own = slice(q * few, (q + 1) * few)
                found = terms_ref[0, table_ref[0, slot], own]
                for r in range(1, local):
                    found += terms_ref[r, table_ref[r, slot], own]
                values.append(found)
            return jnp.concatenate(values, axis=0).astype(BF16)

        out, into = buffer(1, turn, s), buffer(2, turn, s)
        at = (ROUNDS + turn) * STREAMS + s

        def some(chunk, carry):
            steps = [chunk * group + i for i in range(group)]
            parts = [part(peer(step)) for step in steps]
            for step, value in zip(steps, parts):
                out[peer(step)] = value
            for step in steps:
                send(out.at[peer(step)], into, peer(step), at).start()
            return carry

        lax.fori_loop(0, (n - 1) // group, some, 0, unroll=unroll)
        into[me] = part(me)

    @pl.when(leads)
    def _():
        lend.wait_recv()
        begin(1, lent[...])
        broadcast(buffer(0, 0, 1), 1)
        load_factor.wait()
        for level in range(1, LEVELS):
            for s in range(STREAMS):
                step_ahead(level, s)
                if level == ROUNDS:
                    step_back(0, s)
            if level == 1:
                lax.fori_loop(0, total, fill, 0, unroll=4)
                for s in range(STREAMS):
                    for r in range(local):
                        terms_refs[s][r, neighbors] = jnp.zeros((rows, width), F32)
        for turn in range(1, ROUNDS):
            for s in range(STREAMS):
                step_back(turn, s)
        step_back(ROUNDS, 1)
        found_ref[...] = backed[1]
        give_back.start()
        step_back(ROUNDS, 0)
        value = backed[0].astype(F32)
        for r in range(local):
            back_ref[r] = value[r * few : (r + 1) * few].astype(BF16)

        give_near.wait_recv()
        handed = near_in[...].astype(F32)
        for r in range(local):
            near_ref[r, :, : neighbors * width] = handed[r * count : (r + 1) * count].astype(BF16)
        for turn in range(ROUNDS):
            for s in range(STREAMS):
                whole_of(buffer(0, turn, s), turn * STREAMS + s).wait_send()
                whole_of(buffer(1, turn, s), (ROUNDS + turn) * STREAMS + s).wait_send()
        give_back.wait_send()

    @pl.when(helps)
    def _():
        high, low = me // inner, me % inner
        lend.wait_recv()
        pairs[low, high] = jnp.concatenate([stacked, lent[...].astype(F32)], axis=0).astype(BF16)

        def to_far(step, src):
            to = lax.rem(high + step, outer) * inner + low
            return pltpu.make_async_remote_copy(
                src_ref=src,
                dst_ref=src,
                send_sem=send_sem.at[probes_at],
                recv_sem=recv_sem.at[probes_at],
                device_id={"rows": to},
                device_id_type=MESH,
            )

        def to_near(step, src):
            to = high * inner + lax.rem(low + step, inner)
            return pltpu.make_async_remote_copy(
                src_ref=src,
                dst_ref=src,
                send_sem=send_sem.at[probes_at + 1],
                recv_sem=recv_sem.at[probes_at + 1],
                device_id={"rows": to},
                device_id_type=MESH,
            )

        for step in range(1, outer):
            to_far(step, pairs.at[low, high]).start()
        far_all = to_far(1, pairs.at[0, pl.ds(0, outer - 1)])
        far_all.wait_recv()
        for step in range(1, inner):
            to_near(step, pairs.at[low]).start()
        near_all = to_near(1, pairs.at[pl.ds(0, inner - 1)])
        near_all.wait_recv()
        for k in range(neighbors):
            span = slice(k * width, (k + 1) * width)
            theirs = []
            for r in range(local):
                near_ref[r, :, span] = pick_pair(sources[r][k], valids[r][k], 0)
                theirs.append(pick_pair(sources[r][k], valids[r][k], rows).astype(F32))
            near_out[:, span] = jnp.concatenate(theirs, axis=0).astype(BF16)
        give_near.start()
        far_all.wait_send()
        near_all.wait_send()
        give_back.wait_recv()
        value = taken[...].astype(F32)
        for r in range(local):
            back_ref[r] = value[r * few : (r + 1) * few].astype(BF16)
        give_near.wait_send()

    for r in range(local):
        near_ref[r, :, neighbors * width :] = whole[r].astype(BF16)
    lend.wait_send()


def select_kernel(local, count, blocks, back_ref, near_ref, sol_ref, sel_hbm, sel_ref, sems):
    copies = []
    width = back_ref.shape[2]
    for r in range(local):
        value = back_ref[r]
        sol_ref[r] = value
        near = near_ref[r]
        for k in range(blocks):
            product = dot_tn(value, near[:, k * width : (k + 1) * width])
            sel_ref[r, k] = (product / count).astype(BF16)
        copy = pltpu.make_async_copy(sel_ref.at[r], sel_hbm.at[r], sems.at[r])
        copy.start()
        copies.append(copy)
    for copy in copies:
        copy.wait()


def solution(mesh):
    n = mesh.shape["rows"]
    inner = max(d for d in range(1, n + 1) if n % d == 0 and d * d <= n)

    def body(probes, factor, inverses, pattern, owner):
        local, count, width = probes.shape
        neighbors = factor.shape[1]
        total = owner.shape[0]
        rows = local * count
        vmem = pl.BlockSpec(memory_space=pltpu.VMEM)
        anywhere = pl.BlockSpec(memory_space=pl.ANY)
        backed, near = pl.pallas_call(
            functools.partial(solve_kernel, n, inner, local, count, neighbors, total),
            out_shape=(
                jax.ShapeDtypeStruct((local, count, width), BF16),
                jax.ShapeDtypeStruct((local, count, (neighbors + 1) * width), BF16),
            ),
            in_specs=[pl.BlockSpec(memory_space=pltpu.HBM)] * 5,
            out_specs=(vmem, vmem),
            scratch_shapes=[
                pltpu.VMEM(factor.shape, BF16),
                pltpu.VMEM(inverses.shape, BF16),
                pltpu.SMEM((local, total), jnp.int32),
                pltpu.VMEM(probes.shape, BF16),
                pltpu.SMEM((neighbors, total), jnp.int32),
                pltpu.SMEM((total,), jnp.int32),
                pltpu.VMEM((inner, n // inner, 2 * rows, width), BF16),
            ]
            + [pltpu.VMEM((rows, width), BF16)] * 4
            + [pltpu.VMEM((rows, neighbors * width), BF16)] * 2
            + [pltpu.VMEM((local, neighbors + 1, rows, width), F32)] * STREAMS
            + [pltpu.VMEM((n, rows, width), BF16)] * (3 * ROUNDS * STREAMS)
            + [
                pltpu.SemaphoreType.DMA((5,)),
                pltpu.SemaphoreType.DMA((2 * ROUNDS * STREAMS + 5,)),
                pltpu.SemaphoreType.DMA((2 * ROUNDS * STREAMS + 5,)),
            ],
            compiler_params=pltpu.CompilerParams(
                collective_id=0, has_side_effects=True, vmem_limit_bytes=60 * 1024 * 1024
            ),
            name="solve_rounds",
        )(probes, factor, inverses, pattern.T, owner)
        sol, selected = pl.pallas_call(
            functools.partial(select_kernel, local, count, neighbors + 1),
            out_shape=(
                jax.ShapeDtypeStruct((local, count, width), BF16),
                jax.ShapeDtypeStruct((local, neighbors + 1, width, width), BF16),
            ),
            in_specs=[vmem, vmem],
            out_specs=(vmem, anywhere),
            scratch_shapes=[
                pltpu.VMEM((local, neighbors + 1, width, width), BF16),
                pltpu.SemaphoreType.DMA((local,)),
            ],
            compiler_params=pltpu.CompilerParams(vmem_limit_bytes=60 * 1024 * 1024),
            name="select_blocks",
        )(backed, near)
        return sol, selected

    return jax.shard_map(
        body,
        mesh=mesh,
        in_specs=(
            P("rows", "probes", None),
            P("rows", None, None, None),
            P("rows", None, None),
            P(),
            P(),
        ),
        out_specs=(P("rows", "probes", None), P("rows", "probes", None, None)),
        check_vma=False,
    )
```

```python
import functools

import jax
import jax.numpy as jnp
from jax import lax
from jax.experimental import pallas as pl
from jax.experimental.pallas import tpu as pltpu
from jax.sharding import PartitionSpec as P

LEVELS = 4
ROUNDS = LEVELS - 1
STREAMS = 2
MESH = pl.DeviceIdType.MESH
F32 = jnp.float32
BF16 = jnp.bfloat16


def dot_nt(a, b):
    return lax.dot_general(a, b, (((1,), (1,)), ((), ())), preferred_element_type=F32)


def dot_nn(a, b):
    return lax.dot_general(a, b, (((1,), (0,)), ((), ())), preferred_element_type=F32)


def dot_tn(a, b):
    return lax.dot_general(a, b, (((0,), (0,)), ((), ())), preferred_element_type=F32)


def solve_kernel(n, inner, local, count, neighbors, total, *refs):
    probes_hbm, factor_hbm, inv_hbm, pattern_hbm, owner_hbm = refs[:5]
    back_ref, near_ref = refs[5:7]
    scratch = refs[7:]
    factor_ref, inv_ref, factor_t, inv_t, table_ref, probes_ref, pattern_ref, owner_ref = scratch[:8]
    pairs, own_probes, lent, found_ref, taken, near_out, near_in = scratch[8:15]
    terms_refs = scratch[15 : 15 + STREAMS]
    buffers = scratch[15 + STREAMS : 15 + STREAMS * (1 + 3 * ROUNDS)]
    load_sem, send_sem, recv_sem = scratch[15 + STREAMS * (1 + 3 * ROUNDS) :]
    outer = n // inner

    def buffer(kind, turn, s):
        return buffers[(kind * ROUNDS + turn) * STREAMS + s]

    unroll = n <= 16
    group = max(g for g in range(1, 6) if (n - 1) % g == 0)
    width = probes_ref.shape[2]
    few = count
    rows = local * few
    probes_at = 2 * ROUNDS * STREAMS
    lend_at, return_at, near_at = probes_at + 2, probes_at + 3, probes_at + 4
    me = lax.axis_index("rows")
    core = lax.axis_index("probes")
    leads = core % 2 == 1
    helps = core % 2 == 0
    partner = core + 1 - 2 * (core % 2)

    load_inv = pltpu.make_async_copy(inv_hbm, inv_ref, load_sem.at[0])
    load_factor = pltpu.make_async_copy(factor_hbm, factor_ref, load_sem.at[1])
    load_probes = pltpu.make_async_copy(probes_hbm, probes_ref, load_sem.at[2])
    load_pattern = pltpu.make_async_copy(pattern_hbm, pattern_ref, load_sem.at[3])
    load_owner = pltpu.make_async_copy(owner_hbm, owner_ref, load_sem.at[4])
    load_probes.start()

    @pl.when(leads)
    def _():
        load_inv.start()

    load_pattern.start()
    load_owner.start()

    @pl.when(leads)
    def _():
        load_factor.start()

    def peer(step):
        odd = step % 2
        away = n // 2 + odd * ((step + 1) // 2) - (1 - odd) * (step // 2)
        return lax.rem(me + away, n)

    barrier = pltpu.get_barrier_semaphore()

    def greet(step, carry):
        pl.semaphore_signal(barrier, inc=1, device_id={"rows": peer(step)}, device_id_type=MESH)
        return carry

    lax.fori_loop(0, n - 1, greet, 0, unroll=unroll)
    pl.semaphore_signal(barrier, inc=1, device_id={"probes": partner}, device_id_type=MESH)

    own_row = lax.broadcasted_iota(jnp.int32, (rows, width), 0) // few

    def merge(values):
        result = values[0]
        for r in range(1, local):
            result = jnp.where(own_row == r, values[r], result)
        return result

    def turned(value, places):
        places = places % local
        if places == 0:
            return value
        cut = places * few
        return jnp.concatenate([value[cut:], value[:cut]], axis=0)

    def pick(block, at, r, valid):
        value = turned(block, local - r)
        for q in range(1, local):
            value = jnp.where(at == q, turned(block, q - r + local), value)
        return jnp.where(valid, value, jnp.zeros_like(value)).astype(BF16)

    def pick_pair(slot, valid, first):
        device = lax.div(slot, local)
        block = pairs[lax.rem(device, inner), lax.div(device, inner)].astype(F32)
        at = lax.rem(slot, local)
        value = block[first : first + count]
        for r in range(1, local):
            low_row = first + r * count
            value = jnp.where(at == r, block[low_row : low_row + count], value)
        return jnp.where(valid, value, jnp.zeros_like(value)).astype(BF16)

    def send(src, dst, to, at):
        return pltpu.make_async_remote_copy(
            src_ref=src,
            dst_ref=dst.at[me],
            send_sem=send_sem.at[at],
            recv_sem=recv_sem.at[at],
            device_id={"rows": to},
            device_id_type=MESH,
        )

    def whole_of(ref, at):
        every = ref.at[pl.ds(0, n - 1)]
        return pltpu.make_async_remote_copy(
            src_ref=every,
            dst_ref=every,
            send_sem=send_sem.at[at],
            recv_sem=recv_sem.at[at],
            device_id={"rows": peer(0)},
            device_id_type=MESH,
        )

    def broadcast(ref, at, first=0, last=n - 1):
        def one(step, carry):
            send(ref.at[me], ref, peer(step), at).start()
            return carry

        lax.fori_loop(first, last, one, 0, unroll=unroll)

    def pass_on(src, dst, at):
        return pltpu.make_async_remote_copy(
            src_ref=src,
            dst_ref=dst,
            send_sem=send_sem.at[at],
            recv_sem=recv_sem.at[at],
            device_id={"probes": partner},
            device_id_type=MESH,
        )

    lend = pass_on(own_probes, lent, lend_at)
    give_back = pass_on(found_ref, taken, return_at)
    give_near = pass_on(near_out, near_in, near_at)
    load_probes.wait()
    whole = [probes_ref[r].astype(F32) for r in range(local)]
    stacked = jnp.concatenate(whole, axis=0)
    own_probes[...] = stacked.astype(BF16)

    def begin(s, value):
        ended = merge([dot_nt(value, inv_ref[r]) for r in range(local)])
        buffer(0, 0, s)[me] = ended.astype(BF16)

    @pl.when(leads)
    def _():
        load_inv.wait()
        begin(0, stacked.astype(BF16))

    pl.semaphore_wait(barrier, n)

    lend.start()

    @pl.when(leads)
    def _():
        broadcast(buffer(0, 0, 0), 0)

    load_pattern.wait()
    load_owner.wait()

    sources, places, valids = [], [], []
    for r in range(local):
        slot = me * local + r
        row = lax.fori_loop(
            0, total, lambda i, found: jnp.where(owner_ref[i] == slot, i, found), 0, unroll=8
        )
        cols = [pattern_ref[k, row] for k in range(neighbors)]
        valids.append([c >= 0 for c in cols])
        slots = [owner_ref[jnp.maximum(c, 0)] for c in cols]
        sources.append(slots)
        places.append([(lax.div(s, local), lax.rem(s, local)) for s in slots])

    def fill(slot, carry):
        for r in range(local):
            found = neighbors
            for k in range(neighbors):
                here = jnp.logical_and(sources[r][k] == slot, valids[r][k])
                found = jnp.where(here, k, found)
            table_ref[r, slot] = found
        return carry

    solved = [None] * STREAMS
    backed = [None] * STREAMS

    def step_ahead(level, s):
        last = buffer(0, level - 1, s)
        whole_of(last, (level - 1) * STREAMS + s).wait_recv()
        sums = []
        for r in range(local):
            near = []
            for k in range(neighbors):
                device, at = places[r][k]
                near.append(pick(last[device].astype(F32), at, r, valids[r][k]))
            value = dot_nn(jnp.concatenate(near, axis=1), factor_t[r])
            sums.append(value)
        resid = ((lent if s else own_probes)[...].astype(F32) - merge(sums)).astype(BF16)
        solved[s] = merge([dot_nn(resid, inv_t[r]) for r in range(local)])
        if level < ROUNDS:
            ref = buffer(0, level, s)
            ref[me] = solved[s].astype(BF16)
            broadcast(ref, level * STREAMS + s)

    def step_back(turn, s):
        ended = solved[s].astype(BF16).astype(F32)
        if turn > 0:
            into = buffer(2, turn - 1, s)
            whole_of(into, (ROUNDS + turn - 1) * STREAMS + s).wait_recv()
            acc = into[0].astype(F32)
            for d in range(1, n):
                acc += into[d].astype(F32)
            ended = ended - acc
        start = ended.astype(BF16)
        value = merge([dot_nn(start, inv_ref[r]) for r in range(local)]).astype(BF16)
        backed[s] = value
        if turn == ROUNDS:
            return
        terms_ref = terms_refs[s]
        for r in range(local):
            for k in range(neighbors):
                term = dot_nn(value, factor_ref[r, k])
                terms_ref[r, k] = merge([turned(term, r - q + local) for q in range(local)])

        def part(device):
            values = []
            for q in range(local):
                slot = device * local + q
                own = slice(q * few, (q + 1) * few)
                found = terms_ref[0, table_ref[0, slot], own]
                for r in range(1, local):
                    found += terms_ref[r, table_ref[r, slot], own]
                values.append(found)
            return jnp.concatenate(values, axis=0).astype(BF16)

        out, into = buffer(1, turn, s), buffer(2, turn, s)
        at = (ROUNDS + turn) * STREAMS + s

        def some(chunk, carry):
            steps = [chunk * group + i for i in range(group)]
            parts = [part(peer(step)) for step in steps]
            for step, value in zip(steps, parts):
                out[peer(step)] = value
            for step in steps:
                send(out.at[peer(step)], into, peer(step), at).start()
            return carry

        lax.fori_loop(0, (n - 1) // group, some, 0, unroll=unroll)
        into[me] = part(me)

    @pl.when(leads)
    def _():
        lend.wait_recv()
        begin(1, lent[...])
        broadcast(buffer(0, 0, 1), 1)
        load_factor.wait()
        for r in range(local):
            inv_t[r] = inv_ref[r].T
            for k in range(neighbors):
                factor_t[r, k * width : (k + 1) * width] = factor_ref[r, k].T
        for level in range(1, LEVELS):
            for s in range(STREAMS):
                step_ahead(level, s)
                if level == ROUNDS:
                    step_back(0, s)
            if level == 1:
                lax.fori_loop(0, total, fill, 0, unroll=4)
                for s in range(STREAMS):
                    for r in range(local):
                        terms_refs[s][r, neighbors] = jnp.zeros((rows, width), F32)
        for turn in range(1, ROUNDS):
            for s in range(STREAMS):
                step_back(turn, s)
        step_back(ROUNDS, 1)
        found_ref[...] = backed[1]
        give_back.start()
        step_back(ROUNDS, 0)
        value = backed[0].astype(F32)
        for r in range(local):
            back_ref[r] = value[r * few : (r + 1) * few].astype(BF16)

        give_near.wait_recv()
        handed = near_in[...].astype(F32)
        for r in range(local):
            near_ref[r, :, : neighbors * width] = handed[r * count : (r + 1) * count].astype(BF16)
        for turn in range(ROUNDS):
            for s in range(STREAMS):
                whole_of(buffer(0, turn, s), turn * STREAMS + s).wait_send()
                whole_of(buffer(1, turn, s), (ROUNDS + turn) * STREAMS + s).wait_send()
        give_back.wait_send()

    @pl.when(helps)
    def _():
        high, low = me // inner, me % inner
        lend.wait_recv()
        pairs[low, high] = jnp.concatenate([stacked, lent[...].astype(F32)], axis=0).astype(BF16)

        def to_far(step, src):
            to = lax.rem(high + step, outer) * inner + low
            return pltpu.make_async_remote_copy(
                src_ref=src,
                dst_ref=src,
                send_sem=send_sem.at[probes_at],
                recv_sem=recv_sem.at[probes_at],
                device_id={"rows": to},
                device_id_type=MESH,
            )

        def to_near(step, src):
            to = high * inner + lax.rem(low + step, inner)
            return pltpu.make_async_remote_copy(
                src_ref=src,
                dst_ref=src,
                send_sem=send_sem.at[probes_at + 1],
                recv_sem=recv_sem.at[probes_at + 1],
                device_id={"rows": to},
                device_id_type=MESH,
            )

        for step in range(1, outer):
            to_far(step, pairs.at[low, high]).start()
        far_all = to_far(1, pairs.at[0, pl.ds(0, outer - 1)])
        far_all.wait_recv()
        for step in range(1, inner):
            to_near(step, pairs.at[low]).start()
        near_all = to_near(1, pairs.at[pl.ds(0, inner - 1)])
        near_all.wait_recv()
        for k in range(neighbors):
            span = slice(k * width, (k + 1) * width)
            theirs = []
            for r in range(local):
                near_ref[r, :, span] = pick_pair(sources[r][k], valids[r][k], 0)
                theirs.append(pick_pair(sources[r][k], valids[r][k], rows).astype(F32))
            near_out[:, span] = jnp.concatenate(theirs, axis=0).astype(BF16)
        give_near.start()
        far_all.wait_send()
        near_all.wait_send()
        give_back.wait_recv()
        value = taken[...].astype(F32)
        for r in range(local):
            back_ref[r] = value[r * few : (r + 1) * few].astype(BF16)
        give_near.wait_send()

    for r in range(local):
        near_ref[r, :, neighbors * width :] = whole[r].astype(BF16)
    lend.wait_send()


def select_kernel(local, count, blocks, back_ref, near_ref, sol_ref, sel_hbm, sel_ref, sems):
    copies = []
    width = back_ref.shape[2]
    for r in range(local):
        value = back_ref[r]
        sol_ref[r] = value
        near = near_ref[r]
        for k in range(blocks):
            product = dot_tn(value, near[:, k * width : (k + 1) * width])
            sel_ref[r, k] = (product / count).astype(BF16)
        copy = pltpu.make_async_copy(sel_ref.at[r], sel_hbm.at[r], sems.at[r])
        copy.start()
        copies.append(copy)
    for copy in copies:
        copy.wait()


def solution(mesh):
    n = mesh.shape["rows"]
    inner = max(d for d in range(1, n + 1) if n % d == 0 and d * d <= n)

    def body(probes, factor, inverses, pattern, owner):
        local, count, width = probes.shape
        neighbors = factor.shape[1]
        total = owner.shape[0]
        rows = local * count
        vmem = pl.BlockSpec(memory_space=pltpu.VMEM)
        anywhere = pl.BlockSpec(memory_space=pl.ANY)
        backed, near = pl.pallas_call(
            functools.partial(solve_kernel, n, inner, local, count, neighbors, total),
            out_shape=(
                jax.ShapeDtypeStruct((local, count, width), BF16),
                jax.ShapeDtypeStruct((local, count, (neighbors + 1) * width), BF16),
            ),
            in_specs=[pl.BlockSpec(memory_space=pltpu.HBM)] * 5,
            out_specs=(vmem, vmem),
            scratch_shapes=[
                pltpu.VMEM(factor.shape, BF16),
                pltpu.VMEM(inverses.shape, BF16),
                pltpu.VMEM((local, neighbors * width, width), BF16),
                pltpu.VMEM(inverses.shape, BF16),
                pltpu.SMEM((local, total), jnp.int32),
                pltpu.VMEM(probes.shape, BF16),
                pltpu.SMEM((neighbors, total), jnp.int32),
                pltpu.SMEM((total,), jnp.int32),
                pltpu.VMEM((inner, n // inner, 2 * rows, width), BF16),
            ]
            + [pltpu.VMEM((rows, width), BF16)] * 4
            + [pltpu.VMEM((rows, neighbors * width), BF16)] * 2
            + [pltpu.VMEM((local, neighbors + 1, rows, width), F32)] * STREAMS
            + [pltpu.VMEM((n, rows, width), BF16)] * (3 * ROUNDS * STREAMS)
            + [
                pltpu.SemaphoreType.DMA((5,)),
                pltpu.SemaphoreType.DMA((2 * ROUNDS * STREAMS + 5,)),
                pltpu.SemaphoreType.DMA((2 * ROUNDS * STREAMS + 5,)),
            ],
            compiler_params=pltpu.CompilerParams(
                collective_id=0, has_side_effects=True, vmem_limit_bytes=60 * 1024 * 1024
            ),
            name="solve_rounds",
        )(probes, factor, inverses, pattern.T, owner)
        sol, selected = pl.pallas_call(
            functools.partial(select_kernel, local, count, neighbors + 1),
            out_shape=(
                jax.ShapeDtypeStruct((local, count, width), BF16),
                jax.ShapeDtypeStruct((local, neighbors + 1, width, width), BF16),
            ),
            in_specs=[vmem, vmem],
            out_specs=(vmem, anywhere),
            scratch_shapes=[
                pltpu.VMEM((local, neighbors + 1, width, width), BF16),
                pltpu.SemaphoreType.DMA((local,)),
            ],
            compiler_params=pltpu.CompilerParams(vmem_limit_bytes=60 * 1024 * 1024),
            name="select_blocks",
        )(backed, near)
        return sol, selected

    return jax.shard_map(
        body,
        mesh=mesh,
        in_specs=(
            P("rows", "probes", None),
            P("rows", None, None, None),
            P("rows", None, None),
            P(),
            P(),
        ),
        out_specs=(P("rows", "probes", None), P("rows", "probes", None, None)),
        check_vma=False,
    )
```
